32 devices in a mesh: wave: 4 (over z), lev: 2 (over y), grp: 4 (over x, core).
Axes of the slice: x: 2, y: 2, z: 4, core: 2. Of those that a mesh axis runs over, the one named last changes fastest.
Arguments:
- spectra: bfloat16 [2, 4, 2, 16, 1024], P(None, None, 'lev', ('wave', 'grp')), may hold values from -6 to 6
- legendre: bfloat16 [16, 1024, 64], P(('wave', 'grp')), may hold values from -0.1875 to 0.1875
- wavenumbers: int32 [16], replicated, may hold values from 0 to 1023, as said below
- quad_weights: float32 [64], replicated, may hold values from 0.5 to 2
- tracers: float32 [8, 2, 64, 4096], P(None, 'lev', ('wave', 'grp')), may hold values from 0.2 to 2
- kinetics: float32 [8, 8], replicated, may hold values from -2 to 2
- photolysis: float32 [8], replicated, may hold values from -1 to 1
- heat_weights: float32 [3, 8], replicated, may hold values from -2 to 2
Outputs:
- tracers_out: float32 [8, 2, 64, 4096], P(None, 'lev', ('wave', 'grp'))
- heating_spectra: float32 [2, 3, 2, 16, 1024], P(None, None, 'lev', ('wave', 'grp'))
The draws below stay inside these ranges and needn't reach their ends.
Inputs may be any that keep to these rules, and one draw needn't show every extreme that they name: `wavenumbers`: ascending and distinct; slot s holds a value from s * (64) to (s + 1) * 64 - 1.
All inputs are finite; a program needn't handle non-finite values.
Results may differ from the reference program's by a relative error of at most 0.0025.
Values sent between devices are 32-bit elements; how exact they have to be, the bound alone decides.
No kernel may reach another device: no remote copies, remote signals or barrier semaphores. Data moves between devices by JAX's collectives and lax.ppermute only.
A program may use at most 64 MiB of HBM per device.

```python
import math
import jax
import jax.numpy as jnp
from jax import lax

NDEG = 1024
NLON = 4096
FIELDS = 4
TRACERS = 8
HEATS = 3
LEVELS = 2
MW = 16
LATW = 64


def draw_wavenumbers(key, part):
    spacing = NDEG // MW
    offsets = jax.random.randint(jax.random.fold_in(key, 7), (MW,), 0, spacing, dtype=jnp.int32)
    return (jnp.arange(MW, dtype=jnp.int32) * spacing + offsets).astype(jnp.int32)


def block_levels(rng, shape, pieces, least, top_value):
    level, own = 1.0, jax.random.fold_in(rng, 6)
    for position, parts in pieces:
        heights = jnp.exp(jax.random.uniform(jax.random.fold_in(own, position), (parts,), jnp.float32, least / len(pieces), top_value / len(pieces)))
        level = level * jnp.repeat(heights, shape[position] // parts).reshape([-1 if axis == position else 1 for axis in range(len(shape))])
    return level


def gaussian(own_key, extent, width, most, pieces=(), held_as=jnp.bfloat16):
    drawn = width * jax.random.normal(own_key, extent, jnp.float32)
    if pieces:
        drawn = drawn * block_levels(own_key, extent, pieces, -0.22, 0.18)
    return jnp.clip(drawn, -most, most).astype(held_as)


def setup_inputs(seed: int = 0) -> dict:
    arg_keys = jax.random.split(jax.random.key(seed), 9)
    return {
        "spectra": gaussian(arg_keys[0], (2, FIELDS, LEVELS, MW, NDEG), 1.0, 6.0, ((2, 2), (3, 16))),
        "legendre": gaussian(arg_keys[1], (MW, NDEG, LATW), NDEG ** -0.5, 0.1875, ((0, 16),)),
        "wavenumbers": draw_wavenumbers(jax.random.fold_in(arg_keys[8], 71), 0),
        "quad_weights": jnp.clip(jnp.exp(jax.random.uniform(arg_keys[3], (LATW,), jnp.float32, math.log(0.5), math.log(2.0))), 0.5, 2.0),
        "tracers": jnp.clip(jnp.exp(math.log(2.0) - 2.3025851 * jax.random.uniform(arg_keys[4], (TRACERS, LEVELS, LATW, NLON), jnp.float32) ** block_levels(arg_keys[4], (TRACERS, LEVELS, LATW, NLON), ((1, 2), (2, 16)), -0.2, 0.2)), 0.2, 2.0),
        "kinetics": gaussian(arg_keys[5], (TRACERS, TRACERS), TRACERS ** -0.5, 2.0, (), jnp.float32),
        "photolysis": jnp.clip(jax.random.uniform(arg_keys[6], (TRACERS,), jnp.float32, -1.0, 1.0), -1.0, 1.0),
        "heat_weights": gaussian(arg_keys[7], (HEATS, TRACERS), TRACERS ** -0.5, 2.0, (), jnp.float32),
    }


highest = lax.Precision.HIGHEST

def fourier_table(wavenumbers):
    longitudes = jnp.arange(NLON, dtype=jnp.int32)
    phase_index = wavenumbers[:, None] * longitudes[None, :] % NLON
    angles = phase_index.astype(jnp.float32) * (2.0 * math.pi / NLON)
    return jnp.stack([jnp.cos(angles), -jnp.sin(angles)])

def advect(padded, courant_x, courant_y):
    centre = padded[..., 1:-1, :]
    northern = padded[..., :-2, :]
    southern = padded[..., 2:, :]
    western = jnp.roll(centre, 1, axis=-1)
    eastern = jnp.roll(centre, -1, axis=-1)
    return centre - jnp.maximum(courant_x, 0.0) * (centre - western) - jnp.minimum(courant_x, 0.0) * (eastern - centre) - jnp.maximum(courant_y, 0.0) * (centre - northern) - jnp.minimum(courant_y, 0.0) * (southern - centre)

def react(tracer_now, react_rate, photo_rate, kinetics, photolysis):
    mixed = jnp.tensordot(kinetics, tracer_now, axes=1, precision=highest)
    yields = photolysis.reshape((-1,) + (1,) * (tracer_now.ndim - 1))
    return tracer_now + 0.2 * react_rate * mixed + 0.2 * photo_rate * yields * tracer_now[0]

def reference(spectra, legendre, wavenumbers, quad_weights, tracers, kinetics, photolysis, heat_weights):
    degree_mask = jnp.arange(NDEG, dtype=jnp.int32)[None, :] < (NDEG - wavenumbers)[:, None]
    masked_coeffs = jnp.where(degree_mask, spectra.astype(jnp.float32), jnp.zeros((), jnp.float32))
    legendre_wide = legendre.astype(jnp.float32)
    fourier = jnp.einsum('pflsj,sjy->pflsy', masked_coeffs, legendre_wide, precision=highest)
    shared_table = fourier_table(wavenumbers)
    grid_fields = jnp.einsum('pflsy,psx->flyx', fourier, shared_table, precision=highest) * (1.0 / math.sqrt(MW))
    courant_x = 0.45 * jnp.tanh(grid_fields[0])
    courant_y = 0.45 * jnp.tanh(grid_fields[1])
    react_rate = jnp.exp(0.3 * grid_fields[2])
    running_sum = jnp.cumsum(tracers[0], axis=0)
    overhead = jnp.concatenate([jnp.zeros_like(running_sum[:1]), running_sum[:-1]], axis=0)
    photo_rate = jnp.exp(-2.0 * overhead / LEVELS)
    tracer_now = tracers
    for substep in range(2):
        padded = jnp.pad(tracer_now, ((0, 0), (0, 0), (1, 1), (0, 0)))
        tracer_now = react(advect(padded, courant_x, courant_y), react_rate, photo_rate, kinetics, photolysis)
    heating = jnp.tensordot(heat_weights, tracer_now, axes=1, precision=highest) * (1.0 + 0.5 * jnp.tanh(grid_fields[3]))
    heat_fourier = jnp.einsum('klyx,psx->pklsy', heating, shared_table, precision=highest) * (1.0 / math.sqrt(NLON))
    weighted = (heat_fourier * quad_weights).astype(jnp.bfloat16)
    heating_spectra = jnp.einsum('pklsy,sjy->pklsj', weighted.astype(jnp.float32), legendre_wide, precision=highest)
    heating_spectra = jnp.where(degree_mask, heating_spectra, jnp.zeros((), jnp.float32))
    return (tracer_now, heating_spectra)
```

```python
import functools
import math

import jax
import jax.numpy as jnp
from jax import lax
from jax.experimental import pallas as pl
from jax.experimental.pallas import tpu as pltpu
from jax.sharding import PartitionSpec as P

LANES = 128
SUB = 8
PLACE = ("wave", "grp")
VMEM_BYTES = 48 * 1024 * 1024


def split_bf16(value):
    high = value.astype(jnp.bfloat16)
    low = (value - high.astype(jnp.float32)).astype(jnp.bfloat16)
    return high, low


def call(body, out_shape, in_spaces, scratch=(), out_spaces=None, flops=1_000_000):
    shapes = out_shape if isinstance(out_shape, (list, tuple)) else (out_shape,)
    spaces = out_spaces or [pltpu.VMEM] * len(shapes)
    specs = [pl.BlockSpec(memory_space=s) for s in spaces]
    return pl.pallas_call(
        body,
        out_shape=out_shape,
        in_specs=[pl.BlockSpec(memory_space=s) for s in in_spaces],
        out_specs=specs if isinstance(out_shape, (list, tuple)) else specs[0],
        scratch_shapes=list(scratch),
        compiler_params=pltpu.CompilerParams(vmem_limit_bytes=VMEM_BYTES),
        cost_estimate=pl.CostEstimate(flops=flops, bytes_accessed=0, transcendentals=0),
    )


def fourier_kernel(waves_ref, spectra_ref, legendre_ref, out_ref, padded):
    parts, fields, degrees = spectra_ref.shape
    lats = legendre_ref.shape[0]
    places = out_ref.shape[0]
    band = lats // places
    margin = (SUB - band) // 2
    place = lax.axis_index(PLACE)
    limit = degrees - waves_ref[place]
    keep = lax.broadcasted_iota(jnp.int32, (SUB, degrees), 1) < limit
    rows = []
    for p in range(parts):
        block = spectra_ref[p].astype(jnp.float32)
        for f in range(fields):
            row = jnp.broadcast_to(block[f : f + 1], (SUB, degrees))
            rows.append(jnp.where(keep, row, 0.0))
    spread = jnp.concatenate(rows, axis=0).astype(jnp.bfloat16)
    fourier = lax.dot_general(
        legendre_ref[...], spread, (((1,), (1,)), ((), ())), preferred_element_type=jnp.float32
    )
    width = fourier.shape[1]
    padded[...] = jnp.zeros_like(padded)
    padded[SUB : SUB + lats, :width] = fourier
    lane = lax.broadcasted_iota(jnp.int32, (places, LANES), 1) % SUB
    total = jnp.zeros((places, LANES), jnp.float32)
    for r in range(SUB):
        rows_r = padded[pl.ds(SUB - margin + r, places, stride=band), :]
        total = jnp.where(lane == r, rows_r, total)
    out_ref[...] = total


def halo_kernel(width, tracers_ref, near_ref, far_ref):
    parity = lax.axis_index(PLACE) % 2
    band = tracers_ref.shape[1]
    tracers = tracers_ref[...]
    top = tracers[:, :width]
    bottom = tracers[:, band - width :]
    even = parity == 0
    near_ref[...] = jnp.where(even, bottom, top)
    far_ref[...] = jnp.where(even, top, bottom)


def band_kernel(tracers_ref, near_ref, far_ref, padded_ref, column_ref):
    even = lax.axis_index(PLACE) % 2 == 0
    lons = tracers_ref.shape[2]
    near, far = near_ref[...], far_ref[...]
    north = jnp.where(even, far, near)
    south = jnp.where(even, near, far)
    whole = jnp.concatenate([north, tracers_ref[...], south], axis=1)
    padded_ref[:, :, LANES : LANES + lons] = whole
    padded_ref[:, :, :LANES] = whole[:, :, lons - LANES :]
    padded_ref[:, :, LANES + lons :] = whole[:, :, :LANES]
    column_ref[...] = whole[0]


def table_kernel(waves_ref, table_ref):
    lons = table_ref.shape[1]
    waves = table_ref.shape[0] // 4
    row = lax.broadcasted_iota(jnp.int32, (waves, LANES), 0)
    column = lax.broadcasted_iota(jnp.int32, (waves, LANES), 1)
    numbers = jnp.zeros((waves, LANES), jnp.int32)
    for s in range(waves):
        numbers = jnp.where(row == s, waves_ref[s], numbers)

    def turn(longitude):
        index = (numbers * longitude) & (lons - 1)
        angle = index.astype(jnp.float32) * (2.0 * math.pi / lons)
        return jnp.cos(angle), jnp.sin(angle)

    blocks = [turn(column)]
    while len(blocks) * LANES < lons:
        step_cos, step_sin = turn(jnp.full_like(column, len(blocks) * LANES))
        blocks += [(c * step_cos - s * step_sin, s * step_cos + c * step_sin) for c, s in blocks]
    for b, (cosine, sine) in enumerate(blocks):
        span = slice(b * LANES, (b + 1) * LANES)
        cos_high, cos_low = split_bf16(cosine)
        sin_high, sin_low = split_bf16(-sine)
        table_ref[0:waves, span] = cos_high
        table_ref[waves : 2 * waves, span] = sin_high
        table_ref[2 * waves : 3 * waves, span] = cos_low
        table_ref[3 * waves :, span] = sin_low


def grid_kernel(
    levels,
    band,
    kinetics_ref,
    photolysis_ref,
    weights_ref,
    received_ref,
    padded_ref,
    overhead_ref,
    table_ref,
    tracers_ref,
    sent_ref,
    middle,
    coeffs,
    heat,
):
    tracers = padded_ref.shape[0]
    lons = table_ref.shape[1]
    places, waves = received_ref.shape[0], table_ref.shape[0] // 4
    heats = weights_ref.shape[0]
    margin = (SUB - band) // 2
    chunk = 2 * LANES
    fields = 4
    rows = fields * SUB
    turned = received_ref[...].T
    lhs = jnp.concatenate([turned[:rows], turned[rows : 2 * rows]], axis=1) * (
        1.0 / math.sqrt(waves)
    )
    high, low = split_bf16(lhs)
    both = jnp.concatenate(
        [
            jnp.concatenate([high, high], axis=1),
            jnp.concatenate([low, jnp.zeros_like(low)], axis=1),
        ],
        axis=0,
    )
    place = lax.axis_index(PLACE)
    latitude = (
        place * band - margin + lax.broadcasted_iota(jnp.int32, (SUB, chunk), 0)
    )
    inside = (latitude >= 0) & (latitude < places * band)

    def stencil(load, columns, coef, mix):
        west_c, east_c, north_c, south_c, own_c, react, photo = coef
        moved = []
        for t in range(tracers):
            wide = load(t)
            span = wide.shape[1]
            west = pltpu.roll(wide, 1, 1)[:, LANES : LANES + chunk]
            east = pltpu.roll(wide, span - 1, 1)[:, LANES : LANES + chunk]
            own = wide[:, LANES : LANES + chunk]
            north = pltpu.roll(own, 1, 0)
            south = pltpu.roll(own, SUB - 1, 0)
            moved.append(
                own_c * own + west_c * west + east_c * east + north_c * north + south_c * south
            )
        lit = photo * moved[0]
        out = []
        for i in range(tracers):
            mixed = kinetics_ref[i, 0] * moved[0]
            for j in range(1, tracers):
                mixed = mixed + kinetics_ref[i, j] * moved[j]
            out.append(moved[i] + react * mixed + photolysis_ref[i] * lit)
        return out

    def first(step, carry):
        start = pl.multiple_of(step * chunk, chunk)
        grid = jnp.dot(
            both, table_ref[:, pl.ds(start, chunk)], preferred_element_type=jnp.float32
        )
        grid = grid[:rows] + grid[rows:]
        courant_x = jnp.where(inside, 0.45 * jnp.tanh(grid[0:SUB]), 0.0)
        courant_y = jnp.where(inside, 0.45 * jnp.tanh(grid[SUB : 2 * SUB]), 0.0)
        react = 0.2 * jnp.exp(0.3 * grid[2 * SUB : 3 * SUB])
        warm = 1.0 + 0.5 * jnp.tanh(grid[3 * SUB :])
        photo = 0.2 * jnp.exp((-2.0 / levels) * overhead_ref[:, pl.ds(start, chunk)])
        own_c = jnp.where(inside, 1.0 - jnp.abs(courant_x) - jnp.abs(courant_y), 0.0)
        coef = (
            jnp.maximum(courant_x, 0.0),
            -jnp.minimum(courant_x, 0.0),
            jnp.maximum(courant_y, 0.0),
            -jnp.minimum(courant_y, 0.0),
            own_c,
            react,
            photo,
        )
        for n, value in enumerate(coef + (warm,)):
            coeffs[n, :, pl.ds(start, chunk)] = value
        out = stencil(lambda t: padded_ref[t, :, pl.ds(start, chunk + 2 * LANES)], chunk, coef, 0)
        for t in range(tracers):
            middle[t, :, pl.ds(start + LANES, chunk)] = out[t]
        return carry

    lax.fori_loop(0, lons // chunk, first, 0)
    for t in range(tracers):
        middle[t, :, 0:LANES] = middle[t, :, lons : lons + LANES]
        middle[t, :, LANES + lons :] = middle[t, :, LANES : 2 * LANES]

    def second(step, carry):
        start = pl.multiple_of(step * chunk, chunk)
        coef = tuple(coeffs[n, :, pl.ds(start, chunk)] for n in range(7))
        warm = coeffs[7, :, pl.ds(start, chunk)]
        out = stencil(lambda t: middle[t, :, pl.ds(start, chunk + 2 * LANES)], chunk, coef, 0)
        for t in range(tracers):
            tracers_ref[t, :, pl.ds(start, chunk)] = out[t][margin : margin + band]
        heated = []
        for k in range(heats):
            total = weights_ref[k, 0] * out[0]
            for i in range(1, tracers):
                total = total + weights_ref[k, i] * out[i]
            heated.append(total * warm)
        heated = jnp.concatenate(heated, axis=0)
        heat_high, heat_low = split_bf16(heated)
        stacked = jnp.concatenate([heat_high, heat_low], axis=0)
        return carry + lax.dot_general(
            table_ref[:, pl.ds(start, chunk)],
            stacked,
            (((1,), (1,)), ((), ())),
            preferred_element_type=jnp.float32,
        )

    wide = heats * SUB
    total = lax.fori_loop(
        0, lons // chunk, second, jnp.zeros((4 * waves, 2 * wide), jnp.float32)
    )
    heat[...] = jnp.zeros_like(heat)
    heat[:, 0 : 2 * wide] = total
    total = heat[...]
    half = 2 * waves
    total = total[:half] + total[half:] + pltpu.roll(total[:half], LANES - wide, 1)
    lane = lax.broadcasted_iota(jnp.int32, (waves, LANES), 1)
    sent_ref[...] = (
        jnp.where(
            lane < LANES // 2, total[:waves], pltpu.roll(total[waves:], LANES // 2, 1)
        )
        * (1.0 / math.sqrt(lons))
    )


def spectra_kernel(band, heats, waves_ref, received_ref, quad_ref, legendre_ref, out_ref, spread):
    lats, degrees = legendre_ref.shape
    places = received_ref.shape[0]
    margin = (SUB - band) // 2
    place = lax.axis_index(PLACE)
    limit = degrees - waves_ref[place]
    received = received_ref[...]
    for r in range(band):
        spread[pl.ds(r, places, stride=band), :] = pltpu.roll(received, LANES - margin - r, 1)
    weighted = (spread[...].T * quad_ref[...]).astype(jnp.bfloat16)
    out = jnp.dot(weighted, legendre_ref[...], preferred_element_type=jnp.float32)
    keep = lax.broadcasted_iota(jnp.int32, (1, degrees), 1) < limit
    for p in range(2):
        for k in range(heats):
            at = p * (LANES // 2) + k * SUB
            out_ref[p, k, 0] = jnp.where(keep, out[at : at + 1], 0.0)


def body(spectra, legendre, wavenumbers, quad_weights, tracers, kinetics, photolysis, heat_weights):
    places = lax.axis_size(PLACE)
    levels = lax.axis_size("lev")
    count, _, band, lons = tracers.shape
    waves = wavenumbers.shape[0]
    heats = heat_weights.shape[0]
    lats, degrees = legendre.shape[2], legendre.shape[1]
    width = (SUB - band) // 2
    f32 = jnp.float32
    VM, SM = pltpu.VMEM, pltpu.SMEM
    legendre_t = legendre[0].T
    own = tracers[:, 0]

    edge = jax.ShapeDtypeStruct((count, width, lons), f32)
    near, far = call(functools.partial(halo_kernel, width), (edge, edge), [VM])(own)
    near = lax.ppermute(near, PLACE, [(i, i ^ 1) for i in range(places)])
    far = lax.ppermute(
        far, PLACE, [(i, ((i + 1) ^ 1) - 1) for i in range(1, places - 1)]
    )
    sent = call(
        fourier_kernel,
        jax.ShapeDtypeStruct((places, LANES), f32),
        [SM, VM, VM],
        [pltpu.VMEM((lats + 2 * SUB, LANES), f32)],
    )(wavenumbers, spectra[:, :, 0, 0], legendre_t)
    received = lax.all_to_all(sent, PLACE, 0, 0, tiled=True)

    padded, column = call(
        band_kernel,
        (
            jax.ShapeDtypeStruct((count, SUB, lons + 2 * LANES), f32),
            jax.ShapeDtypeStruct((SUB, lons), f32),
        ),
        [VM, VM, VM],
    )(own, near, far)
    overhead = lax.ppermute(column, "lev", [(i, i + 1) for i in range(levels - 1)])
    reach = 1
    while reach < levels - 1:
        overhead = overhead + lax.ppermute(
            overhead, "lev", [(i, i + reach) for i in range(levels - reach)]
        )
        reach *= 2
    table = call(
        table_kernel, jax.ShapeDtypeStruct((4 * waves, lons), jnp.bfloat16), [SM]
    )(wavenumbers)

    tracers_out, heat_sent = call(
        functools.partial(grid_kernel, levels, band),
        (
            jax.ShapeDtypeStruct((count, band, lons), f32),
            jax.ShapeDtypeStruct((waves, LANES), f32),
        ),
        [SM, SM, SM, VM, VM, VM, VM],
        [
            pltpu.VMEM((count, SUB, lons + 2 * LANES), f32),
            pltpu.VMEM((8, SUB, lons), f32),
            pltpu.VMEM((4 * waves, LANES), f32),
        ],
    )(kinetics, photolysis, heat_weights, received, padded, overhead, table)
    heat_received = lax.all_to_all(heat_sent, PLACE, 0, 0, tiled=True)
    heating_spectra = call(
        functools.partial(spectra_kernel, band, heats),
        jax.ShapeDtypeStruct((2, heats, 1, 1, degrees), f32),
        [SM, VM, VM, VM],
        [pltpu.VMEM((lats, LANES), f32)],
    )(wavenumbers, heat_received, quad_weights.reshape(1, lats), legendre_t)
    return (tracers_out[:, None], heating_spectra)


def solution(mesh):
    return jax.shard_map(
        body,
        mesh=mesh,
        in_specs=(
            P(None, None, "lev", ("wave", "grp"), None),
            P(("wave", "grp"), None, None),
            P(),
            P(),
            P(None, "lev", ("wave", "grp"), None),
            P(),
            P(),
            P(),
        ),
        out_specs=(
            P(None, "lev", ("wave", "grp"), None),
            P(None, None, "lev", ("wave", "grp"), None),
        ),
        check_vma=False,
    )
```

```python
import functools
import math

import jax
import jax.numpy as jnp
from jax import lax
from jax.experimental import pallas as pl
from jax.experimental.pallas import tpu as pltpu
from jax.sharding import PartitionSpec as P

LANES = 128
SUB = 8
PLACE = ("wave", "grp")
VMEM_BYTES = 48 * 1024 * 1024
f32 = jnp.float32
bf16 = jnp.bfloat16


def split_bf16(value):
    high = value.astype(bf16)
    return high, value - high.astype(f32)


def call(body, out_shape, in_spaces, scratch=(), flops=1_000_000):
    several = isinstance(out_shape, (list, tuple))
    spec = pl.BlockSpec(memory_space=pltpu.VMEM)
    return pl.pallas_call(
        body,
        out_shape=out_shape,
        in_specs=[pl.BlockSpec(memory_space=s) for s in in_spaces],
        out_specs=[spec] * len(out_shape) if several else spec,
        scratch_shapes=list(scratch),
        compiler_params=pltpu.CompilerParams(vmem_limit_bytes=VMEM_BYTES),
        cost_estimate=pl.CostEstimate(flops=flops, bytes_accessed=0, transcendentals=0),
    )


def fold(tracers):
    count, band, lons = tracers.shape
    cut = tracers.reshape(count, band, lons // LANES, LANES)
    return cut.transpose(0, 2, 1, 3).reshape(-1, LANES)


def unfold(flat, count, band):
    cut = flat.reshape(count, -1, band, LANES)
    return cut.transpose(0, 2, 1, 3).reshape(count, band, -1)


def row_slices(flat_rows, count, band, t, r):
    each = flat_rows // count
    wide = each // band // SUB
    return [pl.ds(t * each + j * band + r, SUB, stride=wide * band) for j in range(wide)]


def load_row(ref, count, band, t, r):
    parts = [ref[s, :] for s in row_slices(ref.shape[0], count, band, t, r)]
    return jnp.concatenate(parts, axis=1)


def store_row(ref, count, band, t, r, value):
    for j, s in enumerate(row_slices(ref.shape[0], count, band, t, r)):
        ref[s, :] = value[:, j * LANES : (j + 1) * LANES]


def shift(row, forward):
    span = row.shape[1]
    lane = lax.broadcasted_iota(jnp.int32, row.shape, 1)
    if forward:
        moved = pltpu.roll(row, 1, 1)
        edge = pltpu.roll(moved[:, :LANES], 1, 0)
        head = jnp.where(lane[:, :LANES] == 0, edge, moved[:, :LANES])
        return jnp.concatenate([head, moved[:, LANES:]], axis=1)
    moved = pltpu.roll(row, span - 1, 1)
    edge = pltpu.roll(moved[:, span - LANES :], SUB - 1, 0)
    last = lane[:, :LANES] == LANES - 1
    tail = jnp.where(last, edge, moved[:, span - LANES :])
    return jnp.concatenate([moved[:, : span - LANES], tail], axis=1)


def fourier_kernel(waves_ref, spectra_ref, legendre_ref, out_ref, padded):
    parts, fields, degrees = spectra_ref.shape
    lats = legendre_ref.shape[0]
    places = out_ref.shape[0]
    band = lats // places
    margin = (SUB - band) // 2
    place = lax.axis_index(PLACE)
    limit = degrees - waves_ref[place]
    keep = lax.broadcasted_iota(jnp.int32, (SUB, degrees), 1) < limit
    rows = []
    for p in range(parts):
        block = spectra_ref[p].astype(f32)
        for f in range(fields):
            row = jnp.broadcast_to(block[f : f + 1], (SUB, degrees))
            rows.append(jnp.where(keep, row, 0.0))
    spread = jnp.concatenate(rows, axis=0).astype(bf16)
    fourier = lax.dot_general(
        legendre_ref[...], spread, (((1,), (1,)), ((), ())), preferred_element_type=f32
    )
    width = fourier.shape[1]
    padded[...] = jnp.zeros_like(padded)
    padded[SUB : SUB + lats, :width] = fourier
    lane = lax.broadcasted_iota(jnp.int32, (places, LANES), 1) % SUB
    total = jnp.zeros((places, LANES), f32)
    for r in range(SUB):
        rows_r = padded[pl.ds(SUB - margin + r, places, stride=band), :]
        total = jnp.where(lane == r, rows_r, total)
    out_ref[...] = total


def edges_kernel(count, band, width, flat_ref, near_ref, far_ref, near_top_ref, far_top_ref):
    even = lax.axis_index(PLACE) % 2 == 0

    def fill(near_first, far_first, near_edge, far_edge):
        for t in range(count):
            for r in range(width):
                near_ref[t, r] = load_row(flat_ref, count, band, t, near_first + r)
                far_ref[t, r] = load_row(flat_ref, count, band, t, far_first + r)
        near_top_ref[...] = load_row(flat_ref, count, band, 0, near_edge)
        far_top_ref[...] = load_row(flat_ref, count, band, 0, far_edge)

    @pl.when(even)
    def _():
        fill(band - width, 0, band - 1, 0)

    @pl.when(jnp.logical_not(even))
    def _():
        fill(0, band - width, 0, band - 1)


def table_kernel(waves_ref, table_ref, turn_ref):
    span = table_ref.shape[1]
    waves = table_ref.shape[0] // 8
    lons = span * SUB
    row = lax.broadcasted_iota(jnp.int32, (waves, LANES), 0)
    column = lax.broadcasted_iota(jnp.int32, (waves, LANES), 1)
    numbers = jnp.zeros((waves, LANES), jnp.int32)
    wide = 8 * waves
    slot = lax.broadcasted_iota(jnp.int32, (SUB, wide), 1) % waves
    by_lane = jnp.zeros((SUB, wide), jnp.int32)
    for s in range(waves):
        numbers = jnp.where(row == s, waves_ref[s], numbers)
        by_lane = jnp.where(slot == s, waves_ref[s], by_lane)

    def wheel(product):
        angle = (product % lons).astype(f32) * (2.0 * math.pi / lons)
        return jnp.cos(angle), jnp.sin(angle)

    sub = lax.broadcasted_iota(jnp.int32, (SUB, wide), 0)
    turn_ref[0], turn_ref[1] = wheel(by_lane * sub * span)

    blocks = [wheel(numbers * column)]
    while len(blocks) * LANES < span:
        step_cos, step_sin = wheel(numbers * (len(blocks) * LANES))
        blocks += [(c * step_cos - s * step_sin, s * step_cos + c * step_sin) for c, s in blocks]
    for b, (cosine, sine) in enumerate(blocks[: span // LANES]):
        columns = slice(b * LANES, (b + 1) * LANES)
        both = split_bf16(cosine) + split_bf16(-sine)
        for n, part in enumerate((0, 2, 1, 3) * 2):
            table_ref[n * waves : (n + 1) * waves, columns] = both[part].astype(bf16)


def ready_kernel(
    levels,
    count,
    band,
    flat_ref,
    near_ref,
    far_ref,
    above_ref,
    near_top_ref,
    far_top_ref,
    cells_ref,
    west_ref,
    east_ref,
    photo_ref,
):
    even = lax.axis_index(PLACE) % 2 == 0
    width = near_ref.shape[1]

    def fill(north, south, north_top, south_top):
        for t in range(count):
            rows = [north[t, r] for r in range(width)]
            rows += [load_row(flat_ref, count, band, t, r) for r in range(band)]
            rows += [south[t, r] for r in range(width)]
            for r, row in enumerate(rows):
                cells_ref[t, r] = row
            for r in range(band + 2):
                row = rows[r + width - 1]
                west_ref[t, r] = shift(row, True)
                east_ref[t, r] = shift(row, False)
        above = [north_top[...]]
        above += [load_row(above_ref, 1, band, 0, r) for r in range(band)]
        above += [south_top[...]]
        for r, row in enumerate(above):
            photo_ref[r] = 0.2 * jnp.exp(row * (-2.0 / levels))

    @pl.when(even)
    def _():
        fill(far_ref, near_ref, far_top_ref, near_top_ref)

    @pl.when(jnp.logical_not(even))
    def _():
        fill(near_ref, far_ref, near_top_ref, far_top_ref)


def grid_kernel(
    kinetics_ref,
    photolysis_ref,
    weights_ref,
    received_ref,
    cells_ref,
    west_ref,
    east_ref,
    photo_ref,
    table_ref,
    turn_ref,
    flat_ref,
    sent_ref,
    middle,
    coeffs,
):
    count, depth, _, span = cells_ref.shape
    rows = west_ref.shape[1]
    band = rows - 2
    margin = (SUB - band) // 2
    halo = (depth - band) // 2
    waves = table_ref.shape[0] // 8
    heats = weights_ref.shape[0]
    fields = 4
    lons = span * SUB
    place = lax.axis_index(PLACE)
    places = lax.axis_size(PLACE)

    lane = lax.broadcasted_iota(jnp.int32, (SUB, 8 * waves), 1)
    real = (lane // waves) % 2 == 0
    turn_cos, turn_sin = turn_ref[0], turn_ref[1]
    scale = 1.0 / math.sqrt(waves)
    turn_a = jnp.where(real, turn_cos, turn_sin) * scale
    turn_b = jnp.where(real, -turn_sin, turn_cos) * scale
    turned = jnp.concatenate([received_ref[...]] * 8, axis=0).T
    wanted = [(f, r) for f in range(fields - 1) for r in range(-1, band + 1)]
    wanted += [(fields - 1, r) for r in range(band)]
    left = []
    for f, r in wanted:
        at = f * SUB + margin + r
        re = turned[at : at + 1]
        im = turned[fields * SUB + at : fields * SUB + at + 1]
        left.append(re * turn_a + im * turn_b)
    left = jnp.concatenate(left, axis=0)
    high, low = split_bf16(left)
    whole_lane = lax.broadcasted_iota(jnp.int32, left.shape, 1)
    left = jnp.where(whole_lane < 4 * waves, high.astype(f32), low).astype(bf16)
    grid = jnp.dot(left, table_ref[...], preferred_element_type=f32)

    for r in range(rows):
        across = grid[r * SUB : (r + 1) * SUB]
        along = grid[(rows + r) * SUB : (rows + r + 1) * SUB]
        warmth = grid[(2 * rows + r) * SUB : (2 * rows + r + 1) * SUB]
        courant_x = 0.45 * jnp.tanh(across)
        courant_y = 0.45 * jnp.tanh(along)
        own = 1.0 - jnp.abs(courant_x) - jnp.abs(courant_y)
        if r == 0 or r == rows - 1:
            inside = (place > 0) if r == 0 else (place < places - 1)
            courant_x = jnp.where(inside, courant_x, 0.0)
            courant_y = jnp.where(inside, courant_y, 0.0)
            own = jnp.where(inside, own, 0.0)
        coeffs[0, r] = own
        coeffs[1, r] = jnp.maximum(courant_x, 0.0)
        coeffs[2, r] = -jnp.minimum(courant_x, 0.0)
        coeffs[3, r] = jnp.maximum(courant_y, 0.0)
        coeffs[4, r] = -jnp.minimum(courant_y, 0.0)
        coeffs[5, r] = 0.2 * jnp.exp(0.3 * warmth)

    def react(moved, r):
        lit = photo_ref[r] * moved[0]
        rate = coeffs[5, r]
        out = []
        for i in range(count):
            mixed = kinetics_ref[i, 0] * moved[0]
            for j in range(1, count):
                mixed = mixed + kinetics_ref[i, j] * moved[j]
            out.append(moved[i] + rate * mixed + photolysis_ref[i] * lit)
        return out

    for r in range(rows):
        moved = []
        for t in range(count):
            at = r + halo - 1
            moved.append(
                coeffs[0, r] * cells_ref[t, at]
                + coeffs[1, r] * west_ref[t, r]
                + coeffs[2, r] * east_ref[t, r]
                + coeffs[3, r] * cells_ref[t, at - 1]
                + coeffs[4, r] * cells_ref[t, at + 1]
            )
        for t, value in enumerate(react(moved, r)):
            middle[t, r] = value

    first = 3 * rows * SUB
    heated = [[None] * band for _ in range(heats)]
    for r in range(band):
        moved = []
        for t in range(count):
            row = middle[t, r + 1]
            moved.append(
                coeffs[0, r + 1] * row
                + coeffs[1, r + 1] * shift(row, True)
                + coeffs[2, r + 1] * shift(row, False)
                + coeffs[3, r + 1] * middle[t, r]
                + coeffs[4, r + 1] * middle[t, r + 2]
            )
        out = react(moved, r + 1)
        for t in range(count):
            store_row(flat_ref, count, band, t, r, out[t])
        warm = 1.0 + 0.5 * jnp.tanh(grid[first + r * SUB : first + (r + 1) * SUB])
        for k in range(heats):
            total = weights_ref[k, 0] * out[0]
            for i in range(1, count):
                total = total + weights_ref[k, i] * out[i]
            heated[k][r] = total * warm

    heat = jnp.concatenate([row for group in heated for row in group], axis=0)
    high, low = split_bf16(heat)
    nt = (((1,), (1,)), ((), ()))
    by_high = lax.dot_general(high, table_ref[...], nt, preferred_element_type=f32)
    by_low = lax.dot_general(low.astype(bf16), table_ref[...], nt, preferred_element_type=f32)
    wide = 8 * waves
    total = by_high + pltpu.roll(by_high, wide - 2 * waves, 1) + by_low
    sums_a, sums_b = [], []
    for n in range(heats * band):
        part = total[n * SUB : (n + 1) * SUB]
        sums_a.append(jnp.sum(part * turn_cos, axis=0, keepdims=True))
        sums_b.append(jnp.sum(part * turn_sin, axis=0, keepdims=True))
    pad = -len(sums_a) % SUB
    sums_a += [jnp.zeros_like(sums_a[0])] * pad
    sums_b += [jnp.zeros_like(sums_b[0])] * pad
    sums_a = jnp.concatenate(sums_a, axis=0)
    sums_b = jnp.concatenate(sums_b, axis=0)
    other = pltpu.roll(sums_b, wide - waves, 1)
    re = sums_a + other
    im = pltpu.roll(sums_a, wide - waves, 1) - sums_b
    size = re.shape[0]
    filler = jnp.zeros((LANES // 2 - size, wide), f32)
    both = jnp.concatenate([re, filler, im, filler], axis=0) * (1.0 / math.sqrt(lons))
    sent_ref[...] = both.T[:waves]


def spectra_kernel(band, heats, waves_ref, received_ref, quad_ref, legendre_ref, out_ref, spread):
    lats, degrees = legendre_ref.shape
    places = received_ref.shape[0]
    place = lax.axis_index(PLACE)
    limit = degrees - waves_ref[place]
    received = received_ref[...]
    for r in range(band):
        spread[pl.ds(r, places, stride=band), :] = pltpu.roll(received, (LANES - r) % LANES, 1)
    weighted = (spread[...].T * quad_ref[...]).astype(bf16)
    out = jnp.dot(weighted, legendre_ref[...], preferred_element_type=f32)
    keep = lax.broadcasted_iota(jnp.int32, (1, degrees), 1) < limit
    for p in range(2):
        for k in range(heats):
            at = p * (LANES // 2) + k * band
            out_ref[p, k, 0] = jnp.where(keep, out[at : at + 1], 0.0)


def body(spectra, legendre, wavenumbers, quad_weights, tracers, kinetics, photolysis, heat_weights):
    places = lax.axis_size(PLACE)
    levels = lax.axis_size("lev")
    count, _, band, lons = tracers.shape
    waves = wavenumbers.shape[0]
    heats = heat_weights.shape[0]
    lats, degrees = legendre.shape[2], legendre.shape[1]
    width = 2
    span = lons // SUB
    flat_rows = count * band * lons // LANES
    VM, SM = pltpu.VMEM, pltpu.SMEM
    legendre_t = legendre[0].T
    flat = fold(tracers[:, 0])
    shape = jax.ShapeDtypeStruct

    near_pairs = [(i, i ^ 1) for i in range(places)]
    far_pairs = [(i, ((i + 1) ^ 1) - 1) for i in range(1, places - 1)]

    near, far, near_top, far_top = call(
        functools.partial(edges_kernel, count, band, width),
        [shape((count, width, SUB, span), f32)] * 2 + [shape((SUB, span), f32)] * 2,
        [VM],
    )(flat)
    near = lax.ppermute(near, PLACE, near_pairs)
    far = lax.ppermute(far, PLACE, far_pairs)

    own_top = flat[: flat_rows // count]
    if levels == 2:
        full = ("wave", "lev", "grp")
        grps = lax.axis_size("grp")

        def upward(pairs):
            def flat_index(place, level):
                return (place // grps * levels + level) * grps + place % grps

            return [(flat_index(a, 0), flat_index(b, 1)) for a, b in pairs]

        above = lax.ppermute(own_top, full, upward([(i, i) for i in range(places)]))
        near_top = lax.ppermute(near_top, full, upward(near_pairs))
        far_top = lax.ppermute(far_top, full, upward(far_pairs))
    else:

        def over(value):
            value = lax.ppermute(value, "lev", [(i, i + 1) for i in range(levels - 1)])
            reach = 1
            while reach < levels - 1:
                value = value + lax.ppermute(
                    value, "lev", [(i, i + reach) for i in range(levels - reach)]
                )
                reach *= 2
            return value

        above = over(own_top)
        near_top = over(lax.ppermute(near_top, PLACE, near_pairs))
        far_top = over(lax.ppermute(far_top, PLACE, far_pairs))

    sent = call(
        fourier_kernel,
        shape((places, LANES), f32),
        [SM, VM, VM],
        [pltpu.VMEM((lats + 2 * SUB, LANES), f32)],
    )(wavenumbers, spectra[:, :, 0, 0], legendre_t)
    received = lax.all_to_all(sent, PLACE, 0, 0, tiled=True)
    table, turn = call(
        table_kernel,
        [shape((8 * waves, span), bf16), shape((2, SUB, 8 * waves), f32)],
        [SM],
    )(wavenumbers)
    cells, west, east, photo = call(
        functools.partial(ready_kernel, levels, count, band),
        [
            shape((count, band + 2 * width, SUB, span), f32),
            shape((count, band + 2, SUB, span), f32),
            shape((count, band + 2, SUB, span), f32),
            shape((band + 2, SUB, span), f32),
        ],
        [VM] * 6,
    )(flat, near, far, above, near_top, far_top)

    flat_out, heat_sent = call(
        grid_kernel,
        [shape((flat_rows, LANES), f32), shape((waves, LANES), f32)],
        [SM] * 3 + [VM] * 7,
        [
            pltpu.VMEM((count, band + 2, SUB, span), f32),
            pltpu.VMEM((6, band + 2, SUB, span), f32),
        ],
    )(
        kinetics,
        photolysis,
        heat_weights,
        received,
        cells,
        west,
        east,
        photo,
        table,
        turn,
    )
    heat_received = lax.all_to_all(heat_sent, PLACE, 0, 0, tiled=True)
    heating_spectra = call(
        functools.partial(spectra_kernel, band, heats),
        shape((2, heats, 1, 1, degrees), f32),
        [SM, VM, VM, VM],
        [pltpu.VMEM((lats, LANES), f32)],
    )(wavenumbers, heat_received, quad_weights.reshape(1, lats), legendre_t)
    return (unfold(flat_out, count, band)[:, None], heating_spectra)


def solution(mesh):
    return jax.shard_map(
        body,
        mesh=mesh,
        in_specs=(
            P(None, None, "lev", ("wave", "grp"), None),
            P(("wave", "grp"), None, None),
            P(),
            P(),
            P(None, "lev", ("wave", "grp"), None),
            P(),
            P(),
            P(),
        ),
        out_specs=(
            P(None, "lev", ("wave", "grp"), None),
            P(None, None, "lev", ("wave", "grp"), None),
        ),
        check_vma=False,
    )
```

```python
import functools
import math

import jax
import jax.numpy as jnp
from jax import lax
from jax.experimental import pallas as pl
from jax.experimental.pallas import tpu as pltpu
from jax.sharding import PartitionSpec as P

LANES = 128
SUB = 8
PLACE = ("wave", "grp")
VMEM_BYTES = 8 * 1024 * 1024
f32 = jnp.float32
bf16 = jnp.bfloat16


def split_bf16(value):
    high = value.astype(bf16)
    return high, value - high.astype(f32)


def call(body, out_shape, in_spaces, scratch=(), flops=1_000_000):
    several = isinstance(out_shape, (list, tuple))
    spec = pl.BlockSpec(memory_space=pltpu.VMEM)
    return pl.pallas_call(
        body,
        out_shape=out_shape,
        in_specs=[pl.BlockSpec(memory_space=s) for s in in_spaces],
        out_specs=[spec] * len(out_shape) if several else spec,
        scratch_shapes=list(scratch),
        compiler_params=pltpu.CompilerParams(vmem_limit_bytes=VMEM_BYTES),
        cost_estimate=pl.CostEstimate(flops=flops, bytes_accessed=0, transcendentals=0),
    )


def fold(tracers):
    count, band, lons = tracers.shape
    cut = tracers.reshape(count, band, lons // LANES, LANES)
    return cut.transpose(0, 2, 1, 3).reshape(-1, LANES)


def unfold(flat, count, band):
    cut = flat.reshape(count, -1, band, LANES)
    return cut.transpose(0, 2, 1, 3).reshape(count, band, -1)


def row_slices(flat_rows, count, band, t, r):
    each = flat_rows // count
    wide = each // band // SUB
    return [pl.ds(t * each + j * band + r, SUB, stride=wide * band) for j in range(wide)]


def load_row(ref, count, band, t, r):
    parts = [ref[s, :] for s in row_slices(ref.shape[0], count, band, t, r)]
    return jnp.concatenate(parts, axis=1)


def store_row(ref, count, band, t, r, value):
    for s, tile in zip(row_slices(ref.shape[0], count, band, t, r), value):
        ref[s, :] = tile


def shift(row, forward):
    span = row.shape[1]
    lane = lax.broadcasted_iota(jnp.int32, row.shape, 1)
    if forward:
        moved = pltpu.roll(row, 1, 1)
        edge = pltpu.roll(moved[:, :LANES], 1, 0)
        head = jnp.where(lane[:, :LANES] == 0, edge, moved[:, :LANES])
        return jnp.concatenate([head, moved[:, LANES:]], axis=1)
    moved = pltpu.roll(row, span - 1, 1)
    edge = pltpu.roll(moved[:, span - LANES :], SUB - 1, 0)
    last = lane[:, :LANES] == LANES - 1
    tail = jnp.where(last, edge, moved[:, span - LANES :])
    return jnp.concatenate([moved[:, : span - LANES], tail], axis=1)


def first_kernel(
    count,
    band,
    width,
    waves_hbm,
    spectra_hbm,
    legendre_hbm,
    flat_hbm,
    sent_ref,
    masked_ref,
    near_ref,
    far_ref,
    flat_ref,
    waves_ref,
    spectra_ref,
    legendre_ref,
    padded,
    sems,
):
    pairs = (
        (legendre_hbm, legendre_ref),
        (spectra_hbm, spectra_ref),
        (waves_hbm, waves_ref),
        (flat_hbm, flat_ref),
    )
    copies = [pltpu.make_async_copy(a, b, sems.at[n]) for n, (a, b) in enumerate(pairs)]
    for copy in copies:
        copy.start()
    parts, fields, degrees = spectra_ref.shape
    lats = legendre_ref.shape[0]
    places = sent_ref.shape[0]
    margin = (SUB - band) // 2
    place = lax.axis_index(PLACE)
    padded[...] = jnp.zeros_like(padded)
    for copy in copies[:3]:
        copy.wait()
    slot = lax.broadcasted_iota(jnp.int32, waves_ref.shape, 1)
    number = jnp.where(slot == place, waves_ref[...].astype(f32), 0.0)
    limit = degrees - jnp.sum(number, axis=1, keepdims=True)
    degree = lax.broadcasted_iota(jnp.int32, (1, degrees), 1).astype(f32)
    keep = jnp.where(degree < limit, 1.0, 0.0)
    masked = (legendre_ref[...].astype(f32) * keep).astype(bf16)
    masked_ref[...] = masked
    rows = []
    for p in range(parts):
        block = spectra_ref[p].astype(f32)
        rows += [jnp.broadcast_to(block[f : f + 1], (SUB, degrees)) for f in range(fields)]
    spread = jnp.concatenate(rows, axis=0).astype(bf16)
    nt = (((1,), (1,)), ((), ()))
    fourier = lax.dot_general(masked, spread, nt, preferred_element_type=f32)
    copies[3].wait()
    even = lax.axis_index(PLACE) % 2 == 0

    def fill(near_first, far_first):
        for t in range(count):
            for r in range(width):
                near_ref[t, r] = load_row(flat_ref, count, band, t, near_first + r)
                far_ref[t, r] = load_row(flat_ref, count, band, t, far_first + r)

    @pl.when(even)
    def _():
        fill(band - width, 0)

    @pl.when(jnp.logical_not(even))
    def _():
        fill(0, band - width)

    padded[SUB : SUB + lats, : parts * fields * SUB] = fourier
    lane = lax.broadcasted_iota(jnp.int32, (places, LANES), 1) % SUB
    total = jnp.zeros((places, LANES), f32)
    for r in range(SUB):
        rows_r = padded[pl.ds(SUB - margin + r, places, stride=band), :]
        total = jnp.where(lane == r, rows_r, total)
    sent_ref[...] = total


def table_kernel(
    waves_ref, kinetics_ref, photolysis_ref, weights_ref, quad_ref, order_ref, table_ref, turn_ref, rows_ref
):
    span = table_ref.shape[1]
    waves = table_ref.shape[0] // 8
    lons = span * SUB
    row = lax.broadcasted_iota(jnp.int32, (waves, LANES), 0)
    column = lax.broadcasted_iota(jnp.int32, (waves, LANES), 1)
    numbers = jnp.zeros((waves, LANES), jnp.int32)
    wide = 8 * waves
    slot = lax.broadcasted_iota(jnp.int32, (SUB, wide), 1) % waves
    by_lane = jnp.zeros((SUB, wide), jnp.int32)
    for s in range(waves):
        numbers = jnp.where(row == s, waves_ref[s], numbers)
        by_lane = jnp.where(slot == s, waves_ref[s], by_lane)

    def wheel(product):
        angle = (product % lons).astype(f32) * (2.0 * math.pi / lons)
        return jnp.cos(angle), jnp.sin(angle)

    sub = lax.broadcasted_iota(jnp.int32, (SUB, wide), 0)
    turn_ref[0], turn_ref[1] = wheel(by_lane * sub * span)

    blocks = [wheel(numbers * column)]
    while len(blocks) * LANES < span:
        step_cos, step_sin = wheel(numbers * (len(blocks) * LANES))
        blocks += [(c * step_cos - s * step_sin, s * step_cos + c * step_sin) for c, s in blocks]
    for b, (cosine, sine) in enumerate(blocks[: span // LANES]):
        columns = slice(b * LANES, (b + 1) * LANES)
        both = split_bf16(cosine) + split_bf16(-sine)
        for n, part in enumerate((0, 2, 1, 3) * 2):
            table_ref[n * waves : (n + 1) * waves, columns] = both[part].astype(bf16)

    count, heats = kinetics_ref.shape[0], weights_ref.shape[0]
    band = quad_ref.shape[0] // lax.axis_size(PLACE)
    first = lax.axis_index(PLACE) * band
    values = [kinetics_ref[i, j] for i in range(count) for j in range(count)]
    values += [photolysis_ref[i] for i in range(count)]
    values += [weights_ref[k, i] for k in range(heats) for i in range(count)]
    values += [quad_ref[first + r] for k in range(heats) for r in range(band)]
    for n, value in enumerate(values):
        rows_ref[n : n + 1, :] = jnp.full((1, LANES), value, f32)


def ready_kernel(count, band, flat_ref, near_ref, far_ref, order_ref, cells_ref, column_ref):
    even = lax.axis_index(PLACE) % 2 == 0
    width = near_ref.shape[1]

    def fill(north, south):
        for t in range(count):
            rows = [north[t, r] for r in range(width)]
            rows += [load_row(flat_ref, count, band, t, r) for r in range(band)]
            rows += [south[t, r] for r in range(width)]
            for r, row in enumerate(rows):
                cells_ref[t, r] = row
            if t == 0:
                for r in range(band + 2):
                    column_ref[r] = rows[r + width - 1]

    @pl.when(even)
    def _():
        fill(far_ref, near_ref)

    @pl.when(jnp.logical_not(even))
    def _():
        fill(near_ref, far_ref)


def grid_kernel(
    levels,
    heats,
    rows_ref,
    received_ref,
    cells_ref,
    above_ref,
    table_ref,
    turn_ref,
    flat_ref,
    sent_ref,
    middle,
    coeffs,
):
    count, depth, _, span = cells_ref.shape
    rows = above_ref.shape[0]
    band = rows - 2
    margin = (SUB - band) // 2
    halo = (depth - band) // 2
    waves = table_ref.shape[0] // 8
    fields = 4
    lons = span * SUB
    tiles = span // LANES
    place = lax.axis_index(PLACE)
    places = lax.axis_size(PLACE)

    def constant(n):
        return jnp.broadcast_to(rows_ref[n : n + 1, :], (SUB, LANES))

    def kinetics(i, j):
        return constant(i * count + j)

    def photolysis(i):
        return constant(count * count + i)

    def heat_weight(k, i):
        return constant(count * (count + 1 + k) + i)

    def cut(value):
        return [value[:, j * LANES : (j + 1) * LANES] for j in range(tiles)]

    def combine(factors, values):
        total = [factors[0] * tile for tile in values[0]]
        for factor, value in zip(factors[1:], values[1:]):
            total = [old + factor * tile for old, tile in zip(total, value)]
        return total

    lane = lax.broadcasted_iota(jnp.int32, (SUB, 8 * waves), 1)
    real = (lane // waves) % 2 == 0
    turn_cos, turn_sin = turn_ref[0], turn_ref[1]
    scale = 1.0 / math.sqrt(waves)
    turn_a = jnp.where(real, turn_cos, turn_sin) * scale
    turn_b = jnp.where(real, -turn_sin, turn_cos) * scale
    turned = jnp.concatenate([received_ref[...]] * 8, axis=0).T
    wanted = [(f, r) for f in range(fields - 1) for r in range(-1, band + 1)]
    wanted += [(fields - 1, r) for r in range(band)]
    left = []
    for f, r in wanted:
        at = f * SUB + margin + r
        re = turned[at : at + 1]
        im = turned[fields * SUB + at : fields * SUB + at + 1]
        left.append(re * turn_a + im * turn_b)
    left = jnp.concatenate(left, axis=0)
    high, low = split_bf16(left)
    whole_lane = lax.broadcasted_iota(jnp.int32, left.shape, 1)
    left = jnp.where(whole_lane < 4 * waves, high.astype(f32), low).astype(bf16)
    grid = jnp.dot(left, table_ref[...], preferred_element_type=f32)

    for r in range(rows):
        across = grid[r * SUB : (r + 1) * SUB]
        along = grid[(rows + r) * SUB : (rows + r + 1) * SUB]
        warmth = grid[(2 * rows + r) * SUB : (2 * rows + r + 1) * SUB]
        courant_x = 0.45 * jnp.tanh(across)
        courant_y = 0.45 * jnp.tanh(along)
        own = 1.0 - jnp.abs(courant_x) - jnp.abs(courant_y)
        if r == 0 or r == rows - 1:
            inside = (place > 0) if r == 0 else (place < places - 1)
            courant_x = jnp.where(inside, courant_x, 0.0)
            courant_y = jnp.where(inside, courant_y, 0.0)
            own = jnp.where(inside, own, 0.0)
        coeffs[0, r] = own
        coeffs[1, r] = jnp.maximum(courant_x, 0.0)
        coeffs[2, r] = -jnp.minimum(courant_x, 0.0)
        coeffs[3, r] = jnp.maximum(courant_y, 0.0)
        coeffs[4, r] = -jnp.minimum(courant_y, 0.0)
        coeffs[5, r] = 0.2 * jnp.exp(0.3 * warmth)

    def react(moved, r):
        overhead = jnp.where(lax.axis_index("lev") > 0, above_ref[r], 0.0)
        photo = 0.2 * jnp.exp(overhead * (-2.0 / levels))
        lit = cut(photo * moved[0])
        rate = cut(coeffs[5, r])
        moved = [cut(value) for value in moved]
        out = []
        for i in range(count):
            mixed = combine([kinetics(i, j) for j in range(count)], moved)
            source = photolysis(i)
            out.append(
                [
                    moved[i][j] + rate[j] * mixed[j] + source * lit[j]
                    for j in range(tiles)
                ]
            )
        return out

    for r in range(rows):
        moved = []
        for t in range(count):
            at = r + halo - 1
            moved.append(
                coeffs[0, r] * cells_ref[t, at]
                + coeffs[1, r] * shift(cells_ref[t, at], True)
                + coeffs[2, r] * shift(cells_ref[t, at], False)
                + coeffs[3, r] * cells_ref[t, at - 1]
                + coeffs[4, r] * cells_ref[t, at + 1]
            )
        for t, value in enumerate(react(moved, r)):
            middle[t, r] = jnp.concatenate(value, axis=1)

    first = 3 * rows * SUB
    heated = [[None] * band for _ in range(heats)]
    for r in range(band):
        moved = []
        for t in range(count):
            row = middle[t, r + 1]
            moved.append(
                coeffs[0, r + 1] * row
                + coeffs[1, r + 1] * shift(row, True)
                + coeffs[2, r + 1] * shift(row, False)
                + coeffs[3, r + 1] * middle[t, r]
                + coeffs[4, r + 1] * middle[t, r + 2]
            )
        out = react(moved, r + 1)
        for t in range(count):
            store_row(flat_ref, count, band, t, r, out[t])
        warm = 1.0 + 0.5 * jnp.tanh(grid[first + r * SUB : first + (r + 1) * SUB])
        for k in range(heats):
            total = combine([heat_weight(k, i) for i in range(count)], out)
            heated[k][r] = jnp.concatenate(total, axis=1) * warm

    heat = jnp.concatenate([row for group in heated for row in group], axis=0)
    high, low = split_bf16(heat)
    nt = (((1,), (1,)), ((), ()))
    by_high = lax.dot_general(high, table_ref[...], nt, preferred_element_type=f32)
    by_low = lax.dot_general(low.astype(bf16), table_ref[...], nt, preferred_element_type=f32)
    wide = 8 * waves
    total = by_high + pltpu.roll(by_high, wide - 2 * waves, 1) + by_low
    sums_a, sums_b = [], []
    for n in range(heats * band):
        part = total[n * SUB : (n + 1) * SUB]
        sums_a.append(jnp.sum(part * turn_cos, axis=0, keepdims=True))
        sums_b.append(jnp.sum(part * turn_sin, axis=0, keepdims=True))
    pad = -len(sums_a) % SUB
    sums_a += [jnp.zeros_like(sums_a[0])] * pad
    sums_b += [jnp.zeros_like(sums_b[0])] * pad
    sums_a = jnp.concatenate(sums_a, axis=0)
    sums_b = jnp.concatenate(sums_b, axis=0)
    other = pltpu.roll(sums_b, wide - waves, 1)
    re = sums_a + other
    im = pltpu.roll(sums_a, wide - waves, 1) - sums_b
    size = re.shape[0]
    first = count * (count + 1 + heats)
    quad = rows_ref[first : first + size, :][:, :1]
    both = jnp.concatenate([re, im], axis=0) * (1.0 / math.sqrt(lons))
    both = both * jnp.concatenate([quad, quad], axis=0)
    filler = jnp.zeros((LANES - 2 * size, wide), f32)
    sent_ref[...] = jnp.concatenate([both, filler], axis=0).T[:waves]


def spectra_kernel(band, heats, received_ref, legendre_ref, out_ref, spread):
    places = received_ref.shape[0]
    received = received_ref[...]
    for r in range(band):
        spread[pl.ds(r, places, stride=band), :] = pltpu.roll(received, (LANES - r) % LANES, 1)
    size = -(-heats * band // SUB) * SUB
    weighted = spread[...].T[: 2 * size].astype(bf16)
    out = jnp.dot(weighted, legendre_ref[...], preferred_element_type=f32)
    for p in range(2):
        for k in range(heats):
            at = p * size + k * band
            out_ref[p, k, 0] = out[at : at + 1]


def body(spectra, legendre, wavenumbers, quad_weights, tracers, kinetics, photolysis, heat_weights):
    places = lax.axis_size(PLACE)
    levels = lax.axis_size("lev")
    count, _, band, lons = tracers.shape
    waves = wavenumbers.shape[0]
    heats = heat_weights.shape[0]
    lats, degrees = legendre.shape[2], legendre.shape[1]
    width = 2
    span = lons // SUB
    flat_rows = count * band * lons // LANES
    VM, SM = pltpu.VMEM, pltpu.SMEM
    legendre_t = legendre[0].T
    flat = fold(tracers[:, 0])
    shape = jax.ShapeDtypeStruct

    near_pairs = [(i, i ^ 1) for i in range(places)]
    far_pairs = [(i, ((i + 1) ^ 1) - 1) for i in range(1, places - 1)]

    sent, masked, near, far, flat = call(
        functools.partial(first_kernel, count, band, width),
        [
            shape((places, LANES), f32),
            shape((lats, degrees), bf16),
            shape((count, width, SUB, span), f32),
            shape((count, width, SUB, span), f32),
            shape((flat_rows, LANES), f32),
        ],
        [pltpu.HBM] * 4,
        [
            pltpu.VMEM((1, waves), jnp.int32),
            pltpu.VMEM((*spectra.shape[:2], degrees), bf16),
            pltpu.VMEM((lats, degrees), bf16),
            pltpu.VMEM((lats + 2 * SUB, LANES), f32),
            pltpu.SemaphoreType.DMA((4,)),
        ],
    )(
        *(
            pltpu.with_memory_space_constraint(x, pltpu.HBM)
            for x in (wavenumbers.reshape(1, waves), spectra[:, :, 0, 0], legendre_t, flat)
        )
    )
    near = lax.ppermute(near, PLACE, near_pairs)
    far = lax.ppermute(far, PLACE, far_pairs)
    received = lax.all_to_all(sent, PLACE, 0, 0, tiled=True)

    constants = count * (count + 1 + heats)
    table, turn, scalars = call(
        table_kernel,
        [
            shape((8 * waves, span), bf16),
            shape((2, SUB, 8 * waves), f32),
            shape((constants + 2 * SUB, LANES), f32),
        ],
        [SM] * 5 + [pl.ANY],
        flops=20_000_000_000,
    )(wavenumbers, kinetics, photolysis, heat_weights, quad_weights, sent)

    cells, column = call(
        functools.partial(ready_kernel, count, band),
        [
            shape((count, band + 2 * width, SUB, span), f32),
            shape((band + 2, SUB, span), f32),
        ],
        [VM] * 3 + [pl.ANY],
    )(flat, near, far, sent)
    above = lax.ppermute(column, "lev", [(i, (i + 1) % levels) for i in range(levels)])
    if levels > 2:
        above = jnp.where(lax.axis_index("lev") > 0, above, 0.0)
    reach = 1
    while reach < levels - 1:
        above = above + lax.ppermute(
            above, "lev", [(i, i + reach) for i in range(levels - reach)]
        )
        reach *= 2

    flat_out, heat_sent = call(
        functools.partial(grid_kernel, levels, heats),
        [shape((flat_rows, LANES), f32), shape((waves, LANES), f32)],
        [VM] * 6,
        [
            pltpu.VMEM((count, band + 2, SUB, span), f32),
            pltpu.VMEM((6, band + 2, SUB, span), f32),
        ],
    )(scalars, received, cells, above, table, turn)
    heat_received = lax.all_to_all(heat_sent, PLACE, 0, 0, tiled=True)
    heating_spectra = call(
        functools.partial(spectra_kernel, band, heats),
        shape((2, heats, 1, 1, degrees), f32),
        [VM, VM],
        [pltpu.VMEM((lats, LANES), f32)],
    )(heat_received, masked)
    return (unfold(flat_out, count, band)[:, None], heating_spectra)


def solution(mesh):
    return jax.shard_map(
        body,
        mesh=mesh,
        in_specs=(
            P(None, None, "lev", ("wave", "grp"), None),
            P(("wave", "grp"), None, None),
            P(),
            P(),
            P(None, "lev", ("wave", "grp"), None),
            P(),
            P(),
            P(),
        ),
        out_specs=(
            P(None, "lev", ("wave", "grp"), None),
            P(None, None, "lev", ("wave", "grp"), None),
        ),
        check_vma=False,
    )
```

```python
import functools
import math

import jax
import jax.numpy as jnp
from jax import lax
from jax.experimental import pallas as pl
from jax.experimental.pallas import tpu as pltpu
from jax.sharding import PartitionSpec as P

LANES = 128
SUB = 8
PLACE = ("wave", "grp")
VMEM_BYTES = 8 * 1024 * 1024
f32 = jnp.float32
bf16 = jnp.bfloat16


def split_bf16(value):
    high = value.astype(bf16)
    return high, value - high.astype(f32)


def call(body, out_shape, in_spaces, scratch=(), flops=1_000_000):
    several = isinstance(out_shape, (list, tuple))
    spec = pl.BlockSpec(memory_space=pltpu.VMEM)
    return pl.pallas_call(
        body,
        out_shape=out_shape,
        in_specs=[pl.BlockSpec(memory_space=s) for s in in_spaces],
        out_specs=[spec] * len(out_shape) if several else spec,
        scratch_shapes=list(scratch),
        compiler_params=pltpu.CompilerParams(vmem_limit_bytes=VMEM_BYTES),
        cost_estimate=pl.CostEstimate(flops=flops, bytes_accessed=0, transcendentals=0),
    )


def fold(tracers):
    count, band, lons = tracers.shape
    cut = tracers.reshape(count, band, lons // LANES, LANES)
    return cut.transpose(0, 2, 1, 3).reshape(-1, LANES)


def unfold(flat, count, band):
    cut = flat.reshape(count, -1, band, LANES)
    return cut.transpose(0, 2, 1, 3).reshape(count, band, -1)


def row_slices(flat_rows, count, band, t, r):
    each = flat_rows // count
    wide = each // band // SUB
    return [pl.ds(t * each + j * band + r, SUB, stride=wide * band) for j in range(wide)]


def load_row(ref, count, band, t, r):
    parts = [ref[s, :] for s in row_slices(ref.shape[0], count, band, t, r)]
    return jnp.concatenate(parts, axis=1)


def store_row(ref, count, band, t, r, value):
    for s, tile in zip(row_slices(ref.shape[0], count, band, t, r), value):
        ref[s, :] = tile


def shift(row, forward):
    span = row.shape[1]
    lane = lax.broadcasted_iota(jnp.int32, row.shape, 1)
    if forward:
        moved = pltpu.roll(row, 1, 1)
        edge = pltpu.roll(moved[:, :LANES], 1, 0)
        head = jnp.where(lane[:, :LANES] == 0, edge, moved[:, :LANES])
        return jnp.concatenate([head, moved[:, LANES:]], axis=1)
    moved = pltpu.roll(row, span - 1, 1)
    edge = pltpu.roll(moved[:, span - LANES :], SUB - 1, 0)
    last = lane[:, :LANES] == LANES - 1
    tail = jnp.where(last, edge, moved[:, span - LANES :])
    return jnp.concatenate([moved[:, : span - LANES], tail], axis=1)


def edges_kernel(
    count,
    band,
    width,
    waves_hbm,
    spectra_hbm,
    legendre_hbm,
    flat_hbm,
    near_ref,
    far_ref,
    waves_ref,
    spectra_ref,
    legendre_ref,
    flat_ref,
    sems,
):
    pairs = (
        (flat_hbm, flat_ref),
        (legendre_hbm, legendre_ref),
        (spectra_hbm, spectra_ref),
        (waves_hbm, waves_ref),
    )
    copies = [pltpu.make_async_copy(a, b, sems.at[n]) for n, (a, b) in enumerate(pairs)]
    for copy in copies:
        copy.start()
    copies[0].wait()
    even = lax.axis_index(PLACE) % 2 == 0

    def fill(near_first, far_first):
        for t in range(count):
            for r in range(width):
                near_ref[t, r] = load_row(flat_ref, count, band, t, near_first + r)
                far_ref[t, r] = load_row(flat_ref, count, band, t, far_first + r)

    @pl.when(even)
    def _():
        fill(band - width, 0)

    @pl.when(jnp.logical_not(even))
    def _():
        fill(0, band - width)

    for copy in copies[1:]:
        copy.wait()


def fourier_kernel(band, waves_ref, spectra_ref, legendre_ref, sent_ref, masked_ref, padded):
    parts, fields, degrees = spectra_ref.shape
    lats = legendre_ref.shape[0]
    places = sent_ref.shape[0]
    margin = (SUB - band) // 2
    place = lax.axis_index(PLACE)
    padded[...] = jnp.zeros_like(padded)
    slot = lax.broadcasted_iota(jnp.int32, waves_ref.shape, 1)
    number = jnp.where(slot == place, waves_ref[...].astype(f32), 0.0)
    limit = degrees - jnp.sum(number, axis=1, keepdims=True)
    degree = lax.broadcasted_iota(jnp.int32, (1, degrees), 1).astype(f32)
    keep = jnp.where(degree < limit, 1.0, 0.0)
    masked = (legendre_ref[...].astype(f32) * keep).astype(bf16)
    masked_ref[...] = masked
    rows = []
    for p in range(parts):
        block = spectra_ref[p].astype(f32)
        rows += [jnp.broadcast_to(block[f : f + 1], (SUB, degrees)) for f in range(fields)]
    spread = jnp.concatenate(rows, axis=0).astype(bf16)
    nt = (((1,), (1,)), ((), ()))
    fourier = lax.dot_general(masked, spread, nt, preferred_element_type=f32)
    padded[SUB : SUB + lats, : parts * fields * SUB] = fourier
    lane = lax.broadcasted_iota(jnp.int32, (places, LANES), 1) % SUB
    total = jnp.zeros((places, LANES), f32)
    for r in range(SUB):
        rows_r = padded[pl.ds(SUB - margin + r, places, stride=band), :]
        total = jnp.where(lane == r, rows_r, total)
    sent_ref[...] = total


def table_kernel(
    waves_ref, kinetics_ref, photolysis_ref, weights_ref, quad_ref, order_ref, table_ref, turn_ref, rows_ref
):
    span = table_ref.shape[1]
    waves = table_ref.shape[0] // 8
    lons = span * SUB
    row = lax.broadcasted_iota(jnp.int32, (waves, LANES), 0)
    column = lax.broadcasted_iota(jnp.int32, (waves, LANES), 1)
    numbers = jnp.zeros((waves, LANES), jnp.int32)
    wide = 8 * waves
    slot = lax.broadcasted_iota(jnp.int32, (SUB, wide), 1) % waves
    by_lane = jnp.zeros((SUB, wide), jnp.int32)
    for s in range(waves):
        numbers = jnp.where(row == s, waves_ref[s], numbers)
        by_lane = jnp.where(slot == s, waves_ref[s], by_lane)

    def wheel(product):
        angle = (product % lons).astype(f32) * (2.0 * math.pi / lons)
        return jnp.cos(angle), jnp.sin(angle)

    sub = lax.broadcasted_iota(jnp.int32, (SUB, wide), 0)
    turn_ref[0], turn_ref[1] = wheel(by_lane * sub * span)

    blocks = [wheel(numbers * column)]
    while len(blocks) * LANES < span:
        step_cos, step_sin = wheel(numbers * (len(blocks) * LANES))
        blocks += [(c * step_cos - s * step_sin, s * step_cos + c * step_sin) for c, s in blocks]
    for b, (cosine, sine) in enumerate(blocks[: span // LANES]):
        columns = slice(b * LANES, (b + 1) * LANES)
        both = split_bf16(cosine) + split_bf16(-sine)
        for n, part in enumerate((0, 2, 1, 3) * 2):
            table_ref[n * waves : (n + 1) * waves, columns] = both[part].astype(bf16)

    count, heats = kinetics_ref.shape[0], weights_ref.shape[0]
    band = quad_ref.shape[0] // lax.axis_size(PLACE)
    first = lax.axis_index(PLACE) * band
    values = [kinetics_ref[i, j] for i in range(count) for j in range(count)]
    values += [photolysis_ref[i] for i in range(count)]
    values += [weights_ref[k, i] for k in range(heats) for i in range(count)]
    values += [quad_ref[first + r] for k in range(heats) for r in range(band)]
    for n, value in enumerate(values):
        rows_ref[n : n + 1, :] = jnp.full((1, LANES), value, f32)


def ready_kernel(count, band, flat_ref, near_ref, far_ref, order_ref, cells_ref, column_ref):
    even = lax.axis_index(PLACE) % 2 == 0
    width = near_ref.shape[1]

    def fill(north, south):
        for t in range(count):
            rows = [north[t, r] for r in range(width)]
            rows += [load_row(flat_ref, count, band, t, r) for r in range(band)]
            rows += [south[t, r] for r in range(width)]
            for r, row in enumerate(rows):
                cells_ref[t, r] = row
            if t == 0:
                for r in range(band + 2):
                    column_ref[r] = rows[r + width - 1]

    @pl.when(even)
    def _():
        fill(far_ref, near_ref)

    @pl.when(jnp.logical_not(even))
    def _():
        fill(near_ref, far_ref)


class Scalars:
    def __init__(self, ref, count, heats):
        self.ref, self.count, self.heats = ref, count, heats

    def row(self, n):
        return jnp.broadcast_to(self.ref[n : n + 1, :], (SUB, LANES))

    def kinetics(self, i, j):
        return self.row(i * self.count + j)

    def photolysis(self, i):
        return self.row(self.count * self.count + i)

    def weight(self, k, i):
        return self.row(self.count * (self.count + 1 + k) + i)

    def quad(self, size):
        first = self.count * (self.count + 1 + self.heats)
        return self.ref[first : first + size, :][:, :1]


def cut(value):
    return [value[:, j : j + LANES] for j in range(0, value.shape[1], LANES)]


def combine(factors, values):
    total = [factors[0] * tile for tile in values[0]]
    for factor, value in zip(factors[1:], values[1:]):
        total = [old + factor * tile for old, tile in zip(total, value)]
    return total


def stencil(coeffs, r, centre, north, south):
    return (
        coeffs[0, r] * centre
        + coeffs[1, r] * shift(centre, True)
        + coeffs[2, r] * shift(centre, False)
        + coeffs[3, r] * north
        + coeffs[4, r] * south
    )


def first_substep_kernel(
    heats,
    rows_ref,
    received_ref,
    cells_ref,
    table_ref,
    turn_ref,
    coeffs_ref,
    base_ref,
    lead_ref,
    warm_ref,
):
    count, depth, _, span = cells_ref.shape
    rows = lead_ref.shape[0]
    band = rows - 2
    margin = (SUB - band) // 2
    halo = (depth - band) // 2
    waves = table_ref.shape[0] // 8
    fields = 4
    place = lax.axis_index(PLACE)
    places = lax.axis_size(PLACE)
    scalars = Scalars(rows_ref, count, heats)

    lane = lax.broadcasted_iota(jnp.int32, (SUB, 8 * waves), 1)
    real = (lane // waves) % 2 == 0
    turn_cos, turn_sin = turn_ref[0], turn_ref[1]
    scale = 1.0 / math.sqrt(waves)
    turn_a = jnp.where(real, turn_cos, turn_sin) * scale
    turn_b = jnp.where(real, -turn_sin, turn_cos) * scale
    turned = jnp.concatenate([received_ref[...]] * 8, axis=0).T
    wanted = [(f, r) for f in range(fields - 1) for r in range(-1, band + 1)]
    wanted += [(fields - 1, r) for r in range(band)]
    left = []
    for f, r in wanted:
        at = f * SUB + margin + r
        re = turned[at : at + 1]
        im = turned[fields * SUB + at : fields * SUB + at + 1]
        left.append(re * turn_a + im * turn_b)
    left = jnp.concatenate(left, axis=0)
    high, low = split_bf16(left)
    whole_lane = lax.broadcasted_iota(jnp.int32, left.shape, 1)
    left = jnp.where(whole_lane < 4 * waves, high.astype(f32), low).astype(bf16)
    grid = jnp.dot(left, table_ref[...], preferred_element_type=f32)

    for r in range(rows):
        across = grid[r * SUB : (r + 1) * SUB]
        along = grid[(rows + r) * SUB : (rows + r + 1) * SUB]
        warmth = grid[(2 * rows + r) * SUB : (2 * rows + r + 1) * SUB]
        courant_x = 0.45 * jnp.tanh(across)
        courant_y = 0.45 * jnp.tanh(along)
        own = 1.0 - jnp.abs(courant_x) - jnp.abs(courant_y)
        if r == 0 or r == rows - 1:
            inside = (place > 0) if r == 0 else (place < places - 1)
            courant_x = jnp.where(inside, courant_x, 0.0)
            courant_y = jnp.where(inside, courant_y, 0.0)
            own = jnp.where(inside, own, 0.0)
        coeffs_ref[0, r] = own
        coeffs_ref[1, r] = jnp.maximum(courant_x, 0.0)
        coeffs_ref[2, r] = -jnp.minimum(courant_x, 0.0)
        coeffs_ref[3, r] = jnp.maximum(courant_y, 0.0)
        coeffs_ref[4, r] = -jnp.minimum(courant_y, 0.0)
        coeffs_ref[5, r] = 0.2 * jnp.exp(0.3 * warmth)
    first = 3 * rows * SUB
    for r in range(band):
        warm_ref[r] = 1.0 + 0.5 * jnp.tanh(grid[first + r * SUB : first + (r + 1) * SUB])

    for r in range(rows):
        at = r + halo - 1
        moved = [
            stencil(coeffs_ref, r, cells_ref[t, at], cells_ref[t, at - 1], cells_ref[t, at + 1])
            for t in range(count)
        ]
        lead_ref[r] = moved[0]
        moved = [cut(value) for value in moved]
        rate = cut(coeffs_ref[5, r])
        for i in range(count):
            mixed = combine([scalars.kinetics(i, j) for j in range(count)], moved)
            out = [a + b * c for a, b, c in zip(moved[i], rate, mixed)]
            base_ref[i, r] = jnp.concatenate(out, axis=1)


def second_substep_kernel(
    levels,
    heats,
    rows_ref,
    above_ref,
    table_ref,
    turn_ref,
    coeffs_ref,
    base_ref,
    lead_ref,
    warm_ref,
    flat_ref,
    sent_ref,
    middle,
):
    count, rows, _, span = base_ref.shape
    band = rows - 2
    waves = table_ref.shape[0] // 8
    lons = span * SUB
    scalars = Scalars(rows_ref, count, heats)
    turn_cos, turn_sin = turn_ref[0], turn_ref[1]
    covered = lax.axis_index("lev") > 0
    photo = []
    for r in range(rows):
        overhead = jnp.where(covered, above_ref[r], 0.0)
        photo.append(0.2 * jnp.exp(overhead * (-2.0 / levels)))
        lit = cut(photo[r] * lead_ref[r])
        for t in range(count):
            source = scalars.photolysis(t)
            parts = [old + source * tile for old, tile in zip(cut(base_ref[t, r]), lit)]
            middle[t, r] = jnp.concatenate(parts, axis=1)

    heated = [[None] * band for _ in range(heats)]
    for r in range(band):
        moved = [
            stencil(coeffs_ref, r + 1, middle[t, r + 1], middle[t, r], middle[t, r + 2])
            for t in range(count)
        ]
        lit = cut(photo[r + 1] * moved[0])
        rate = cut(coeffs_ref[5, r + 1])
        moved = [cut(value) for value in moved]
        out = []
        for i in range(count):
            mixed = combine([scalars.kinetics(i, j) for j in range(count)], moved)
            source = scalars.photolysis(i)
            out.append(
                [a + b * c + source * d for a, b, c, d in zip(moved[i], rate, mixed, lit)]
            )
        for t in range(count):
            store_row(flat_ref, count, band, t, r, out[t])
        for k in range(heats):
            total = combine([scalars.weight(k, i) for i in range(count)], out)
            heated[k][r] = jnp.concatenate(total, axis=1) * warm_ref[r]

    heat = jnp.concatenate([row for group in heated for row in group], axis=0)
    high, low = split_bf16(heat)
    nt = (((1,), (1,)), ((), ()))
    by_high = lax.dot_general(high, table_ref[...], nt, preferred_element_type=f32)
    by_low = lax.dot_general(low.astype(bf16), table_ref[...], nt, preferred_element_type=f32)
    wide = 8 * waves
    total = by_high + pltpu.roll(by_high, wide - 2 * waves, 1) + by_low
    sums_a, sums_b = [], []
    for n in range(heats * band):
        part = total[n * SUB : (n + 1) * SUB]
        sums_a.append(jnp.sum(part * turn_cos, axis=0, keepdims=True))
        sums_b.append(jnp.sum(part * turn_sin, axis=0, keepdims=True))
    pad = -len(sums_a) % SUB
    sums_a += [jnp.zeros_like(sums_a[0])] * pad
    sums_b += [jnp.zeros_like(sums_b[0])] * pad
    sums_a = jnp.concatenate(sums_a, axis=0)
    sums_b = jnp.concatenate(sums_b, axis=0)
    other = pltpu.roll(sums_b, wide - waves, 1)
    re = sums_a + other
    im = pltpu.roll(sums_a, wide - waves, 1) - sums_b
    size = re.shape[0]
    quad = scalars.quad(size)
    both = jnp.concatenate([re, im], axis=0) * (1.0 / math.sqrt(lons))
    both = both * jnp.concatenate([quad, quad], axis=0)
    filler = jnp.zeros((LANES - 2 * size, wide), f32)
    sent_ref[...] = jnp.concatenate([both, filler], axis=0).T[:waves]


def spectra_kernel(band, heats, received_ref, legendre_ref, out_ref, spread):
    places = received_ref.shape[0]
    received = received_ref[...]
    for r in range(band):
        spread[pl.ds(r, places, stride=band), :] = pltpu.roll(received, (LANES - r) % LANES, 1)
    size = -(-heats * band // SUB) * SUB
    weighted = spread[...].T[: 2 * size].astype(bf16)
    out = jnp.dot(weighted, legendre_ref[...], preferred_element_type=f32)
    for p in range(2):
        for k in range(heats):
            at = p * size + k * band
            out_ref[p, k, 0] = out[at : at + 1]


def body(spectra, legendre, wavenumbers, quad_weights, tracers, kinetics, photolysis, heat_weights):
    places = lax.axis_size(PLACE)
    levels = lax.axis_size("lev")
    count, _, band, lons = tracers.shape
    waves = wavenumbers.shape[0]
    heats = heat_weights.shape[0]
    lats, degrees = legendre.shape[2], legendre.shape[1]
    width = 2
    span = lons // SUB
    flat_rows = count * band * lons // LANES
    VM, SM = pltpu.VMEM, pltpu.SMEM
    legendre_t = legendre[0].T
    flat = fold(tracers[:, 0])
    shape = jax.ShapeDtypeStruct

    near_pairs = [(i, i ^ 1) for i in range(places)]
    far_pairs = [(i, ((i + 1) ^ 1) - 1) for i in range(1, places - 1)]

    halo = shape((count, width, SUB, span), f32)
    near, far, waves_in, spectra_in, legendre_in, flat = call(
        functools.partial(edges_kernel, count, band, width),
        [
            halo,
            halo,
            shape((1, waves), jnp.int32),
            shape((*spectra.shape[:2], degrees), bf16),
            shape((lats, degrees), bf16),
            shape((flat_rows, LANES), f32),
        ],
        [pltpu.HBM] * 4,
        [pltpu.SemaphoreType.DMA((4,))],
    )(
        *(
            pltpu.with_memory_space_constraint(x, pltpu.HBM)
            for x in (wavenumbers.reshape(1, waves), spectra[:, :, 0, 0], legendre_t, flat)
        )
    )
    near = lax.ppermute(near, PLACE, near_pairs)
    far = lax.ppermute(far, PLACE, far_pairs)
    sent, masked = call(
        functools.partial(fourier_kernel, band),
        [shape((places, LANES), f32), shape((lats, degrees), bf16)],
        [VM] * 3,
        [pltpu.VMEM((lats + 2 * SUB, LANES), f32)],
        flops=1000000,
    )(waves_in, spectra_in, legendre_in)
    received = lax.all_to_all(sent, PLACE, 0, 0, tiled=True)

    constants = count * (count + 1 + heats)
    table, turn, scalars = call(
        table_kernel,
        [
            shape((8 * waves, span), bf16),
            shape((2, SUB, 8 * waves), f32),
            shape((constants + 2 * SUB, LANES), f32),
        ],
        [SM] * 5 + [pl.ANY],
        flops=20000000000,
    )(wavenumbers, kinetics, photolysis, heat_weights, quad_weights, sent)

    cells, column = call(
        functools.partial(ready_kernel, count, band),
        [
            shape((count, band + 2 * width, SUB, span), f32),
            shape((band + 2, SUB, span), f32),
        ],
        [VM] * 3 + [pl.ANY],
    )(flat, near, far, sent)
    above = lax.ppermute(column, "lev", [(i, (i + 1) % levels) for i in range(levels)])
    if levels > 2:
        above = jnp.where(lax.axis_index("lev") > 0, above, 0.0)
    reach = 1
    while reach < levels - 1:
        above = above + lax.ppermute(
            above, "lev", [(i, i + reach) for i in range(levels - reach)]
        )
        reach *= 2

    field = shape((band + 2, SUB, span), f32)
    coeffs, base, lead, warm = call(
        functools.partial(first_substep_kernel, heats),
        [
            shape((6, band + 2, SUB, span), f32),
            shape((count, band + 2, SUB, span), f32),
            field,
            shape((band, SUB, span), f32),
        ],
        [VM] * 5,
        flops=1000000,
    )(scalars, received, cells, table, turn)
    flat_out, heat_sent = call(
        functools.partial(second_substep_kernel, levels, heats),
        [shape((flat_rows, LANES), f32), shape((waves, LANES), f32)],
        [VM] * 8,
        [pltpu.VMEM((count, band + 2, SUB, span), f32)],
    )(scalars, above, table, turn, coeffs, base, lead, warm)
    heat_received = lax.all_to_all(heat_sent, PLACE, 0, 0, tiled=True)
    heating_spectra = call(
        functools.partial(spectra_kernel, band, heats),
        shape((2, heats, 1, 1, degrees), f32),
        [VM, VM],
        [pltpu.VMEM((lats, LANES), f32)],
    )(heat_received, masked)
    return (unfold(flat_out, count, band)[:, None], heating_spectra)


def solution(mesh):
    return jax.shard_map(
        body,
        mesh=mesh,
        in_specs=(
            P(None, None, "lev", ("wave", "grp"), None),
            P(("wave", "grp"), None, None),
            P(),
            P(),
            P(None, "lev", ("wave", "grp"), None),
            P(),
            P(),
            P(),
        ),
        out_specs=(
            P(None, "lev", ("wave", "grp"), None),
            P(None, None, "lev", ("wave", "grp"), None),
        ),
        check_vma=False,
    )
```

```python
import functools
import math

import jax
import jax.numpy as jnp
from jax import lax
from jax.experimental import pallas as pl
from jax.experimental.pallas import tpu as pltpu
from jax.sharding import PartitionSpec as P

LANES = 128
SUB = 8
PLACE = ("wave", "grp")
VMEM_BYTES = 8 * 1024 * 1024
f32 = jnp.float32
bf16 = jnp.bfloat16


def split_bf16(value):
    high = value.astype(bf16)
    return high, value - high.astype(f32)


def call(body, out_shape, in_spaces, scratch=(), flops=1_000_000, out_space=pltpu.VMEM):
    several = isinstance(out_shape, (list, tuple))
    spec = pl.BlockSpec(memory_space=out_space)
    return pl.pallas_call(
        body,
        out_shape=out_shape,
        in_specs=[pl.BlockSpec(memory_space=s) for s in in_spaces],
        out_specs=[spec] * len(out_shape) if several else spec,
        scratch_shapes=list(scratch),
        compiler_params=pltpu.CompilerParams(vmem_limit_bytes=VMEM_BYTES),
        cost_estimate=pl.CostEstimate(flops=flops, bytes_accessed=0, transcendentals=0),
    )


def fold(tracers):
    count, band, lons = tracers.shape
    cut = tracers.reshape(count, band, lons // LANES, LANES)
    return cut.transpose(0, 2, 1, 3).reshape(-1, LANES)


def unfold(flat, count, band):
    cut = flat.reshape(count, -1, band, LANES)
    return cut.transpose(0, 2, 1, 3).reshape(count, band, -1)


def row_slices(flat_rows, count, band, t, r):
    each = flat_rows // count
    wide = each // band // SUB
    return [pl.ds(t * each + j * band + r, SUB, stride=wide * band) for j in range(wide)]


def load_row(ref, count, band, t, r):
    parts = [ref[s, :] for s in row_slices(ref.shape[0], count, band, t, r)]
    return jnp.concatenate(parts, axis=1)


def store_row(ref, count, band, t, r, value):
    for s, tile in zip(row_slices(ref.shape[0], count, band, t, r), value):
        ref[s, :] = tile


def shift(row, forward):
    span = row.shape[1]
    lane = lax.broadcasted_iota(jnp.int32, row.shape, 1)
    if forward:
        moved = pltpu.roll(row, 1, 1)
        edge = pltpu.roll(moved[:, :LANES], 1, 0)
        head = jnp.where(lane[:, :LANES] == 0, edge, moved[:, :LANES])
        return jnp.concatenate([head, moved[:, LANES:]], axis=1)
    moved = pltpu.roll(row, span - 1, 1)
    edge = pltpu.roll(moved[:, span - LANES :], SUB - 1, 0)
    last = lane[:, :LANES] == LANES - 1
    tail = jnp.where(last, edge, moved[:, span - LANES :])
    return jnp.concatenate([moved[:, : span - LANES], tail], axis=1)


def edges_kernel(
    count,
    band,
    width,
    waves_hbm,
    spectra_hbm,
    legendre_hbm,
    flat_hbm,
    far_ref,
    near_ref,
    waves_ref,
    spectra_ref,
    legendre_ref,
    flat_ref,
    sems,
):
    each = flat_hbm.shape[0] // count
    pairs = [(flat_hbm.at[pl.ds(t * each, each)], flat_ref.at[pl.ds(t * each, each)]) for t in range(count)]
    pairs += [(legendre_hbm, legendre_ref), (spectra_hbm, spectra_ref), (waves_hbm, waves_ref)]
    copies = [pltpu.make_async_copy(a, b, sems.at[n]) for n, (a, b) in enumerate(pairs)]
    for copy in copies:
        copy.start()
    even = lax.axis_index(PLACE) % 2 == 0

    def fill(near_first, far_first):
        for t in range(count):
            copies[t].wait()
            for r in range(width):
                near_ref[t, r] = load_row(flat_ref, count, band, t, near_first + r)
                far_ref[t, r] = load_row(flat_ref, count, band, t, far_first + r)

    @pl.when(even)
    def _():
        fill(band - width, 0)

    @pl.when(jnp.logical_not(even))
    def _():
        fill(0, band - width)

    for copy in copies[count:]:
        copy.wait()


def fourier_kernel(band, waves_ref, spectra_ref, legendre_ref, sent_ref, masked_ref, padded):
    parts, fields, degrees = spectra_ref.shape
    lats = legendre_ref.shape[0]
    places = sent_ref.shape[0]
    margin = (SUB - band) // 2
    place = lax.axis_index(PLACE)
    padded[...] = jnp.zeros_like(padded)
    slot = lax.broadcasted_iota(jnp.int32, waves_ref.shape, 1)
    number = jnp.where(slot == place, waves_ref[...].astype(f32), 0.0)
    limit = degrees - jnp.sum(number, axis=1, keepdims=True)
    degree = lax.broadcasted_iota(jnp.int32, (1, degrees), 1).astype(f32)
    keep = jnp.where(degree < limit, 1.0, 0.0)
    masked = (legendre_ref[...].astype(f32) * keep).astype(bf16)
    masked_ref[...] = masked
    rows = []
    for p in range(parts):
        block = spectra_ref[p].astype(f32)
        rows += [jnp.broadcast_to(block[f : f + 1], (SUB, degrees)) for f in range(fields)]
    spread = jnp.concatenate(rows, axis=0).astype(bf16)
    nt = (((1,), (1,)), ((), ()))
    fourier = lax.dot_general(masked, spread, nt, preferred_element_type=f32)
    padded[SUB : SUB + lats, : parts * fields * SUB] = fourier
    lane = lax.broadcasted_iota(jnp.int32, (places, LANES), 1) % SUB
    total = jnp.zeros((places, LANES), f32)
    for r in range(SUB):
        rows_r = padded[pl.ds(SUB - margin + r, places, stride=band), :]
        total = jnp.where(lane == r, rows_r, total)
    sent_ref[...] = total


def table_kernel(
    waves_ref, kinetics_ref, photolysis_ref, weights_ref, quad_ref, order_ref, table_ref, turned_ref, turn_ref, rows_ref
):
    span = table_ref.shape[1]
    waves = table_ref.shape[0] // 8
    lons = span * SUB
    row = lax.broadcasted_iota(jnp.int32, (waves, LANES), 0)
    column = lax.broadcasted_iota(jnp.int32, (waves, LANES), 1)
    numbers = jnp.zeros((waves, LANES), jnp.int32)
    wide = 8 * waves
    slot = lax.broadcasted_iota(jnp.int32, (SUB, wide), 1) % waves
    by_lane = jnp.zeros((SUB, wide), jnp.int32)
    for s in range(waves):
        numbers = jnp.where(row == s, waves_ref[s], numbers)
        by_lane = jnp.where(slot == s, waves_ref[s], by_lane)

    def wheel(product):
        angle = (product % lons).astype(f32) * (2.0 * math.pi / lons)
        return jnp.cos(angle), jnp.sin(angle)

    sub = lax.broadcasted_iota(jnp.int32, (SUB, wide), 0)
    turn_ref[0], turn_ref[1] = wheel(by_lane * sub * span)

    blocks = [wheel(numbers * column)]
    while len(blocks) * LANES < span:
        step_cos, step_sin = wheel(numbers * (len(blocks) * LANES))
        blocks += [(c * step_cos - s * step_sin, s * step_cos + c * step_sin) for c, s in blocks]
    for b, (cosine, sine) in enumerate(blocks[: span // LANES]):
        columns = slice(b * LANES, (b + 1) * LANES)
        both = split_bf16(cosine) + split_bf16(-sine)
        for n, part in enumerate((0, 2, 1, 3) * 2):
            table_ref[n * waves : (n + 1) * waves, columns] = both[part].astype(bf16)
        stacked = jnp.concatenate([both[part].astype(f32) for part in (0, 2, 1, 3) * 2], axis=0)
        turned_ref[columns, :] = stacked.T.astype(bf16)

    count, heats = kinetics_ref.shape[0], weights_ref.shape[0]
    band = quad_ref.shape[0] // lax.axis_size(PLACE)
    first = lax.axis_index(PLACE) * band
    values = [kinetics_ref[i, j] for i in range(count) for j in range(count)]
    values += [photolysis_ref[i] for i in range(count)]
    values += [weights_ref[k, i] for k in range(heats) for i in range(count)]
    yields = [photolysis_ref[i] for i in range(count)]

    def product(row, column):
        total = row[0] * column[0]
        for a, b in zip(row[1:], column[1:]):
            total = total + a * b
        return total

    mixed = [product([kinetics_ref[i, j] for j in range(count)], yields) for i in range(count)]
    weights = [[weights_ref[k, i] for i in range(count)] for k in range(heats)]
    values += mixed
    values += [product(row, yields) for row in weights]
    values += [product(row, mixed) for row in weights]
    values += [0.0] * (-len(values) % SUB)
    values += [quad_ref[first + r] for k in range(heats) for r in range(band)]
    for n, value in enumerate(values):
        rows_ref[n : n + 1, :] = jnp.full((1, LANES), value, f32)


def ready_kernel(count, band, flat_ref, near_ref, far_ref, order_ref, cells_ref, column_ref):
    even = lax.axis_index(PLACE) % 2 == 0
    width = near_ref.shape[1]

    def fill(north, south):
        for t in range(count):
            rows = [north[t, r] for r in range(width)]
            rows += [load_row(flat_ref, count, band, t, r) for r in range(band)]
            rows += [south[t, r] for r in range(width)]
            for r, row in enumerate(rows):
                cells_ref[t, r] = row
            if t == 0:
                for r in range(band + 2):
                    column_ref[r] = rows[r + width - 1]

    @pl.when(even)
    def _():
        fill(far_ref, near_ref)

    @pl.when(jnp.logical_not(even))
    def _():
        fill(near_ref, far_ref)


def scalar_rows(count, heats):
    rows = count * (count + 2 + heats) + 2 * heats
    return -(-rows // SUB) * SUB


class Scalars:
    def __init__(self, ref, count, heats):
        self.ref, self.count, self.heats = ref, count, heats

    def row(self, n):
        return jnp.broadcast_to(self.ref[n : n + 1, :], (SUB, LANES))

    def kinetics(self, i, j):
        return self.row(i * self.count + j)

    def photolysis(self, i):
        return self.row(self.count * self.count + i)

    def weight(self, k, i):
        return self.row(self.count * (self.count + 1 + k) + i)

    def mixed_yield(self, i):
        return self.row(self.count * (self.count + 1 + self.heats) + i)

    def heat_yield(self, k):
        return self.row(self.count * (self.count + 2 + self.heats) + k)

    def heat_mixed_yield(self, k):
        return self.row(self.count * (self.count + 2 + self.heats) + self.heats + k)

    def quad(self, size):
        first = scalar_rows(self.count, self.heats)
        return self.ref[first : first + size, :][:, :1]


def cut(value):
    return [value[:, j : j + LANES] for j in range(0, value.shape[1], LANES)]


def combine(factors, values):
    total = [factors[0] * tile for tile in values[0]]
    for factor, value in zip(factors[1:], values[1:]):
        total = [old + factor * tile for old, tile in zip(total, value)]
    return total


def stencil(coeffs, r, centre, north, south):
    return (
        coeffs[0, r] * centre
        + coeffs[1, r] * shift(centre, True)
        + coeffs[2, r] * shift(centre, False)
        + coeffs[3, r] * north
        + coeffs[4, r] * south
    )


def substeps_kernel(
    heats,
    rows_ref,
    received_ref,
    cells_ref,
    table_ref,
    turn_ref,
    coeffs_ref,
    base_ref,
    lead_ref,
    second_lead_ref,
    heat_ref,
    warm_ref,
    middle,
):
    count, depth, _, span = cells_ref.shape
    rows = lead_ref.shape[0]
    band = rows - 2
    margin = (SUB - band) // 2
    halo = (depth - band) // 2
    waves = table_ref.shape[0] // 8
    fields = 4
    place = lax.axis_index(PLACE)
    places = lax.axis_size(PLACE)
    scalars = Scalars(rows_ref, count, heats)

    lane = lax.broadcasted_iota(jnp.int32, (SUB, 8 * waves), 1)
    real = (lane // waves) % 2 == 0
    turn_cos, turn_sin = turn_ref[0], turn_ref[1]
    scale = 1.0 / math.sqrt(waves)
    turn_a = jnp.where(real, turn_cos, turn_sin) * scale
    turn_b = jnp.where(real, -turn_sin, turn_cos) * scale
    turned = jnp.concatenate([received_ref[...]] * 8, axis=0).T
    wanted = [(f, r) for f in range(fields - 1) for r in range(-1, band + 1)]
    wanted += [(fields - 1, r) for r in range(band)]
    left = []
    for f, r in wanted:
        at = f * SUB + margin + r
        re = turned[at : at + 1]
        im = turned[fields * SUB + at : fields * SUB + at + 1]
        left.append(re * turn_a + im * turn_b)
    left = jnp.concatenate(left, axis=0)
    high, low = split_bf16(left)
    whole_lane = lax.broadcasted_iota(jnp.int32, left.shape, 1)
    left = jnp.where(whole_lane < 4 * waves, high.astype(f32), low).astype(bf16)
    grid = jnp.dot(left, table_ref[...], preferred_element_type=f32)

    for r in range(rows):
        across = grid[r * SUB : (r + 1) * SUB]
        along = grid[(rows + r) * SUB : (rows + r + 1) * SUB]
        warmth = grid[(2 * rows + r) * SUB : (2 * rows + r + 1) * SUB]
        courant_x = 0.45 * jnp.tanh(across)
        courant_y = 0.45 * jnp.tanh(along)
        own = 1.0 - jnp.abs(courant_x) - jnp.abs(courant_y)
        if r == 0 or r == rows - 1:
            inside = (place > 0) if r == 0 else (place < places - 1)
            courant_x = jnp.where(inside, courant_x, 0.0)
            courant_y = jnp.where(inside, courant_y, 0.0)
            own = jnp.where(inside, own, 0.0)
        coeffs_ref[0, r] = own
        coeffs_ref[1, r] = jnp.maximum(courant_x, 0.0)
        coeffs_ref[2, r] = -jnp.minimum(courant_x, 0.0)
        coeffs_ref[3, r] = jnp.maximum(courant_y, 0.0)
        coeffs_ref[4, r] = -jnp.minimum(courant_y, 0.0)
        coeffs_ref[5, r] = 0.2 * jnp.exp(0.3 * warmth)
    first = 3 * rows * SUB
    for r in range(band):
        warm_ref[r] = 1.0 + 0.5 * jnp.tanh(grid[first + r * SUB : first + (r + 1) * SUB])

    for r in range(rows):
        at = r + halo - 1
        moved = [
            stencil(coeffs_ref, r, cells_ref[t, at], cells_ref[t, at - 1], cells_ref[t, at + 1])
            for t in range(count)
        ]
        lead_ref[r] = moved[0]
        moved = [cut(value) for value in moved]
        rate = cut(coeffs_ref[5, r])
        for i in range(count):
            mixed = combine([scalars.kinetics(i, j) for j in range(count)], moved)
            out = [a + b * c for a, b, c in zip(moved[i], rate, mixed)]
            middle[i, r] = jnp.concatenate(out, axis=1)

    for r in range(band):
        moved = [
            stencil(coeffs_ref, r + 1, middle[t, r + 1], middle[t, r], middle[t, r + 2])
            for t in range(count)
        ]
        second_lead_ref[r] = moved[0]
        moved = [cut(value) for value in moved]
        rate = cut(coeffs_ref[5, r + 1])
        outs = []
        for i in range(count):
            mixed = combine([scalars.kinetics(i, j) for j in range(count)], moved)
            outs.append([a + b * c for a, b, c in zip(moved[i], rate, mixed)])
            base_ref[i, r] = jnp.concatenate(outs[i], axis=1)
        for k in range(heats):
            total = combine([scalars.weight(k, i) for i in range(count)], outs)
            heat_ref[k, r] = jnp.concatenate(total, axis=1)


def analysis_kernel(
    levels,
    count,
    rows_ref,
    above_ref,
    turned_ref,
    turn_ref,
    coeffs_ref,
    lead_ref,
    second_lead_ref,
    heat_ref,
    warm_ref,
    u_ref,
    v_ref,
    sent_ref,
):
    rows, _, span = lead_ref.shape
    band = rows - 2
    heats = heat_ref.shape[0]
    waves = turned_ref.shape[1] // 8
    lons = span * SUB
    scalars = Scalars(rows_ref, count, heats)
    turn_cos, turn_sin = turn_ref[0], turn_ref[1]
    covered = lax.axis_index("lev") > 0
    photo, source = [], []
    for r in range(rows):
        overhead = jnp.where(covered, above_ref[r], 0.0)
        photo.append(0.2 * jnp.exp(overhead * (-2.0 / levels)))
        source.append(photo[r] * lead_ref[r])

    heated = [[None] * band for _ in range(heats)]
    for r in range(band):
        moved = cut(stencil(coeffs_ref, r + 1, source[r + 1], source[r], source[r + 2]))
        rate, light = cut(coeffs_ref[5, r + 1]), cut(photo[r + 1])
        own = scalars.photolysis(0)
        v = [a * b for a, b in zip(rate, moved)]
        lead = cut(second_lead_ref[r])
        u = [m + p * (a + own * m) for m, p, a in zip(moved, light, lead)]
        u_ref[r] = jnp.concatenate(u, axis=1)
        v_ref[r] = jnp.concatenate(v, axis=1)
        for k in range(heats):
            by_u, by_v = scalars.heat_yield(k), scalars.heat_mixed_yield(k)
            parts = cut(heat_ref[k, r])
            parts = [a + by_u * b + by_v * c for a, b, c in zip(parts, u, v)]
            heated[k][r] = jnp.concatenate(parts, axis=1) * warm_ref[r]

    heat = jnp.concatenate([row for group in heated for row in group], axis=0)
    high, low = split_bf16(heat)
    by_high = jnp.dot(high, turned_ref[...], preferred_element_type=f32)
    by_low = jnp.dot(low.astype(bf16), turned_ref[...], preferred_element_type=f32)
    wide = 8 * waves
    total = by_high + pltpu.roll(by_high, wide - 2 * waves, 1) + by_low
    sums_a, sums_b = [], []
    for n in range(heats * band):
        part = total[n * SUB : (n + 1) * SUB]
        sums_a.append(jnp.sum(part * turn_cos, axis=0, keepdims=True))
        sums_b.append(jnp.sum(part * turn_sin, axis=0, keepdims=True))
    pad = -len(sums_a) % SUB
    sums_a += [jnp.zeros_like(sums_a[0])] * pad
    sums_b += [jnp.zeros_like(sums_b[0])] * pad
    sums_a = jnp.concatenate(sums_a, axis=0)
    sums_b = jnp.concatenate(sums_b, axis=0)
    other = pltpu.roll(sums_b, wide - waves, 1)
    re = sums_a + other
    im = pltpu.roll(sums_a, wide - waves, 1) - sums_b
    size = re.shape[0]
    quad = scalars.quad(size)
    both = jnp.concatenate([re, im], axis=0) * (1.0 / math.sqrt(lons))
    both = both * jnp.concatenate([quad, quad], axis=0)
    filler = jnp.zeros((LANES - 2 * size, wide), f32)
    sent_ref[...] = jnp.concatenate([both, filler], axis=0).T[:waves]


def last_kernel(
    band,
    heats,
    received_ref,
    legendre_ref,
    rows_ref,
    base_ref,
    u_ref,
    v_ref,
    spectra_hbm,
    flat_hbm,
    spread,
    spectra_ref,
    flat_ref,
    sems,
):
    places = received_ref.shape[0]
    count = base_ref.shape[0]
    received = received_ref[...]
    for r in range(band):
        spread[pl.ds(r, places, stride=band), :] = pltpu.roll(received, (LANES - r) % LANES, 1)
    size = -(-heats * band // SUB) * SUB
    weighted = spread[...].T[: 2 * size].astype(bf16)
    out = jnp.dot(weighted, legendre_ref[...], preferred_element_type=f32)
    for p in range(2):
        for k in range(heats):
            at = p * size + k * band
            spectra_ref[p, k, 0] = out[at : at + 1]
    copies = [pltpu.make_async_copy(spectra_ref, spectra_hbm, sems.at[count])]
    copies[0].start()
    scalars = Scalars(rows_ref, count, heats)
    each = flat_hbm.shape[0] // count
    for t in range(count):
        by_u, by_v = scalars.photolysis(t), scalars.mixed_yield(t)
        for r in range(band):
            parts = zip(cut(base_ref[t, r]), cut(u_ref[r]), cut(v_ref[r]))
            store_row(flat_ref, count, band, t, r, [a + by_u * b + by_v * c for a, b, c in parts])
        mine = pl.ds(t * each, each)
        copies.append(pltpu.make_async_copy(flat_ref.at[mine], flat_hbm.at[mine], sems.at[t]))
        copies[-1].start()
    for copy in copies:
        copy.wait()


def body(spectra, legendre, wavenumbers, quad_weights, tracers, kinetics, photolysis, heat_weights):
    places = lax.axis_size(PLACE)
    levels = lax.axis_size("lev")
    count, _, band, lons = tracers.shape
    waves = wavenumbers.shape[0]
    heats = heat_weights.shape[0]
    lats, degrees = legendre.shape[2], legendre.shape[1]
    width = 2
    span = lons // SUB
    flat_rows = count * band * lons // LANES
    VM, SM = pltpu.VMEM, pltpu.SMEM
    legendre_t = legendre[0].T
    flat = fold(tracers[:, 0])
    shape = jax.ShapeDtypeStruct

    near_pairs = [(i, i ^ 1) for i in range(places)]
    far_pairs = [(i, ((i + 1) ^ 1) - 1) for i in range(1, places - 1)]

    halo = shape((count, width, SUB, span), f32)
    far, near, waves_in, spectra_in, legendre_in, flat = call(
        functools.partial(edges_kernel, count, band, width),
        [
            halo,
            halo,
            shape((1, waves), jnp.int32),
            shape((*spectra.shape[:2], degrees), bf16),
            shape((lats, degrees), bf16),
            shape((flat_rows, LANES), f32),
        ],
        [pltpu.HBM] * 4,
        [pltpu.SemaphoreType.DMA((count + 3,))],
    )(
        *(
            pltpu.with_memory_space_constraint(x, pltpu.HBM)
            for x in (wavenumbers.reshape(1, waves), spectra[:, :, 0, 0], legendre_t, flat)
        )
    )
    far = lax.ppermute(far, PLACE, far_pairs)
    near = lax.ppermute(near, PLACE, near_pairs)
    sent, masked = call(
        functools.partial(fourier_kernel, band),
        [shape((places, LANES), f32), shape((lats, degrees), bf16)],
        [VM] * 3,
        [pltpu.VMEM((lats + 2 * SUB, LANES), f32)],
        flops=1000000,
    )(waves_in, spectra_in, legendre_in)
    received = lax.all_to_all(sent, PLACE, 0, 0, tiled=True)

    constants = scalar_rows(count, heats)
    table, turned, turn, scalars = call(
        table_kernel,
        [
            shape((8 * waves, span), bf16),
            shape((span, 8 * waves), bf16),
            shape((2, SUB, 8 * waves), f32),
            shape((constants + 2 * SUB, LANES), f32),
        ],
        [SM] * 5 + [pl.ANY],
        flops=20000000000,
    )(wavenumbers, kinetics, photolysis, heat_weights, quad_weights, sent)

    cells, column = call(
        functools.partial(ready_kernel, count, band),
        [
            shape((count, band + 2 * width, SUB, span), f32),
            shape((band + 2, SUB, span), f32),
        ],
        [VM] * 3 + [pl.ANY],
    )(flat, near, far, sent)
    above = lax.ppermute(column, "lev", [(i, (i + 1) % levels) for i in range(levels)])
    if levels > 2:
        above = jnp.where(lax.axis_index("lev") > 0, above, 0.0)
    reach = 1
    while reach < levels - 1:
        above = above + lax.ppermute(
            above, "lev", [(i, i + reach) for i in range(levels - reach)]
        )
        reach *= 2

    inner, outer = (band, SUB, span), (band + 2, SUB, span)
    coeffs, base, lead, second_lead, heat, warm = call(
        functools.partial(substeps_kernel, heats),
        [
            shape((6, *outer), f32),
            shape((count, *inner), f32),
            shape(outer, f32),
            shape(inner, f32),
            shape((heats, *inner), f32),
            shape(inner, f32),
        ],
        [VM] * 5,
        [pltpu.VMEM((count, *outer), f32)],
    )(scalars, received, cells, table, turn)
    u, v, heat_sent = call(
        functools.partial(analysis_kernel, levels, count),
        [shape(inner, f32), shape(inner, f32), shape((waves, LANES), f32)],
        [VM] * 9,
    )(scalars, above, turned, turn, coeffs, lead, second_lead, heat, warm)
    heat_received = lax.all_to_all(heat_sent, PLACE, 0, 0, tiled=True)
    heating_spectra, flat_out = call(
        functools.partial(last_kernel, band, heats),
        [shape((2, heats, 1, 1, degrees), f32), shape((flat_rows, LANES), f32)],
        [VM] * 6,
        [
            pltpu.VMEM((lats, LANES), f32),
            pltpu.VMEM((2, heats, 1, 1, degrees), f32),
            pltpu.VMEM((flat_rows, LANES), f32),
            pltpu.SemaphoreType.DMA((count + 1,)),
        ],
        out_space=pltpu.HBM,
    )(heat_received, masked, scalars, base, u, v)
    return (unfold(flat_out, count, band)[:, None], heating_spectra)


def solution(mesh):
    return jax.shard_map(
        body,
        mesh=mesh,
        in_specs=(
            P(None, None, "lev", ("wave", "grp"), None),
            P(("wave", "grp"), None, None),
            P(),
            P(),
            P(None, "lev", ("wave", "grp"), None),
            P(),
            P(),
            P(),
        ),
        out_specs=(
            P(None, "lev", ("wave", "grp"), None),
            P(None, None, "lev", ("wave", "grp"), None),
        ),
        check_vma=False,
    )
```

```python
import functools
import math

import jax
import jax.numpy as jnp
from jax import lax
from jax.experimental import pallas as pl
from jax.experimental.pallas import tpu as pltpu
from jax.sharding import PartitionSpec as P

LANES = 128
SUB = 8
PLACE = ("wave", "grp")
VMEM_BYTES = 8 * 1024 * 1024
f32 = jnp.float32
bf16 = jnp.bfloat16


def split_bf16(value):
    high = value.astype(bf16)
    return high, value - high.astype(f32)


def call(body, out_shape, in_spaces, scratch=(), flops=1_000_000, out_space=pltpu.VMEM):
    several = isinstance(out_shape, (list, tuple))
    spec = pl.BlockSpec(memory_space=out_space)
    return pl.pallas_call(
        body,
        out_shape=out_shape,
        in_specs=[pl.BlockSpec(memory_space=s) for s in in_spaces],
        out_specs=[spec] * len(out_shape) if several else spec,
        scratch_shapes=list(scratch),
        compiler_params=pltpu.CompilerParams(vmem_limit_bytes=VMEM_BYTES),
        cost_estimate=pl.CostEstimate(flops=flops, bytes_accessed=0, transcendentals=0),
    )


def halves(tracers):
    count, band, lons = tracers.shape
    cut = tracers.reshape(count, 2, band // 2, lons // LANES, LANES)
    return cut.transpose(0, 3, 1, 2, 4).reshape(-1, 2, band // 2, LANES)


def unfold(flat, count, band):
    cut = flat.reshape(count, -1, band, LANES)
    return cut.transpose(0, 2, 1, 3).reshape(count, band, -1)


def row_slices(flat_rows, count, band, t, r):
    each = flat_rows // count
    wide = each // band // SUB
    return [pl.ds(t * each + j * band + r, SUB, stride=wide * band) for j in range(wide)]


def load_row(ref, count, band, t, r):
    parts = [ref[s, :] for s in row_slices(ref.shape[0], count, band, t, r)]
    return jnp.concatenate(parts, axis=1)


def store_row(ref, count, band, t, r, value):
    for s, tile in zip(row_slices(ref.shape[0], count, band, t, r), value):
        ref[s, :] = tile


def shift(row, forward):
    span = row.shape[1]
    lane = lax.broadcasted_iota(jnp.int32, row.shape, 1)
    if forward:
        moved = pltpu.roll(row, 1, 1)
        edge = pltpu.roll(moved[:, :LANES], 1, 0)
        head = jnp.where(lane[:, :LANES] == 0, edge, moved[:, :LANES])
        return jnp.concatenate([head, moved[:, LANES:]], axis=1)
    moved = pltpu.roll(row, span - 1, 1)
    edge = pltpu.roll(moved[:, span - LANES :], SUB - 1, 0)
    last = lane[:, :LANES] == LANES - 1
    tail = jnp.where(last, edge, moved[:, span - LANES :])
    return jnp.concatenate([moved[:, : span - LANES], tail], axis=1)


def edges_kernel(
    waves_hbm,
    spectra_hbm,
    legendre_hbm,
    halves_hbm,
    near_ref,
    far_ref,
    waves_ref,
    spectra_ref,
    legendre_ref,
    sems,
):
    odd = lax.axis_index(PLACE) % 2
    pairs = (
        (halves_hbm.at[:, 1 - odd], near_ref),
        (halves_hbm.at[:, odd], far_ref),
        (legendre_hbm, legendre_ref),
        (spectra_hbm, spectra_ref),
        (waves_hbm, waves_ref),
    )
    copies = [pltpu.make_async_copy(a, b, sems.at[n]) for n, (a, b) in enumerate(pairs)]
    for copy in copies:
        copy.start()
    for copy in copies:
        copy.wait()


def fourier_kernel(band, waves_ref, spectra_ref, legendre_ref, sent_ref, masked_ref, padded):
    parts, fields, degrees = spectra_ref.shape
    lats = legendre_ref.shape[0]
    places = sent_ref.shape[0]
    margin = (SUB - band) // 2
    place = lax.axis_index(PLACE)
    padded[...] = jnp.zeros_like(padded)
    slot = lax.broadcasted_iota(jnp.int32, waves_ref.shape, 1)
    number = jnp.where(slot == place, waves_ref[...].astype(f32), 0.0)
    limit = degrees - jnp.sum(number, axis=1, keepdims=True)
    degree = lax.broadcasted_iota(jnp.int32, (1, degrees), 1).astype(f32)
    keep = jnp.where(degree < limit, 1.0, 0.0)
    masked = (legendre_ref[...].astype(f32) * keep).astype(bf16)
    masked_ref[...] = masked
    rows = []
    for p in range(parts):
        block = spectra_ref[p].astype(f32)
        rows += [jnp.broadcast_to(block[f : f + 1], (SUB, degrees)) for f in range(fields)]
    spread = jnp.concatenate(rows, axis=0).astype(bf16)
    nt = (((1,), (1,)), ((), ()))
    fourier = lax.dot_general(masked, spread, nt, preferred_element_type=f32)
    padded[SUB : SUB + lats, : parts * fields * SUB] = fourier
    lane = lax.broadcasted_iota(jnp.int32, (places, LANES), 1) % SUB
    total = jnp.zeros((places, LANES), f32)
    for r in range(SUB):
        rows_r = padded[pl.ds(SUB - margin + r, places, stride=band), :]
        total = jnp.where(lane == r, rows_r, total)
    sent_ref[...] = total


def table_kernel(
    waves_ref, kinetics_ref, photolysis_ref, weights_ref, quad_ref, order_ref, table_ref, turned_ref, turn_ref, rows_ref
):
    span = table_ref.shape[1]
    waves = table_ref.shape[0] // 8
    lons = span * SUB
    row = lax.broadcasted_iota(jnp.int32, (waves, LANES), 0)
    column = lax.broadcasted_iota(jnp.int32, (waves, LANES), 1)
    numbers = jnp.zeros((waves, LANES), jnp.int32)
    wide = 8 * waves
    slot = lax.broadcasted_iota(jnp.int32, (SUB, wide), 1) % waves
    by_lane = jnp.zeros((SUB, wide), jnp.int32)
    for s in range(waves):
        numbers = jnp.where(row == s, waves_ref[s], numbers)
        by_lane = jnp.where(slot == s, waves_ref[s], by_lane)

    def wheel(product):
        angle = (product % lons).astype(f32) * (2.0 * math.pi / lons)
        return jnp.cos(angle), jnp.sin(angle)

    sub = lax.broadcasted_iota(jnp.int32, (SUB, wide), 0)
    turn_ref[0], turn_ref[1] = wheel(by_lane * sub * span)

    blocks = [wheel(numbers * column)]
    while len(blocks) * LANES < span:
        step_cos, step_sin = wheel(numbers * (len(blocks) * LANES))
        blocks += [(c * step_cos - s * step_sin, s * step_cos + c * step_sin) for c, s in blocks]
    for b, (cosine, sine) in enumerate(blocks[: span // LANES]):
        columns = slice(b * LANES, (b + 1) * LANES)
        both = split_bf16(cosine) + split_bf16(-sine)
        for n, part in enumerate((0, 2, 1, 3) * 2):
            table_ref[n * waves : (n + 1) * waves, columns] = both[part].astype(bf16)
        stacked = jnp.concatenate([both[part].astype(f32) for part in (0, 2, 1, 3) * 2], axis=0)
        turned_ref[columns, :] = stacked.T.astype(bf16)

    count, heats = kinetics_ref.shape[0], weights_ref.shape[0]
    band = quad_ref.shape[0] // lax.axis_size(PLACE)
    first = lax.axis_index(PLACE) * band
    values = [kinetics_ref[i, j] for i in range(count) for j in range(count)]
    values += [photolysis_ref[i] for i in range(count)]
    values += [weights_ref[k, i] for k in range(heats) for i in range(count)]
    yields = [photolysis_ref[i] for i in range(count)]

    def product(row, column):
        total = row[0] * column[0]
        for a, b in zip(row[1:], column[1:]):
            total = total + a * b
        return total

    mixed = [product([kinetics_ref[i, j] for j in range(count)], yields) for i in range(count)]
    weights = [[weights_ref[k, i] for i in range(count)] for k in range(heats)]
    values += mixed
    values += [product(row, yields) for row in weights]
    values += [product(row, mixed) for row in weights]
    values += [0.0] * (-len(values) % SUB)
    values += [quad_ref[first + r] for k in range(heats) for r in range(band)]
    for n, value in enumerate(values):
        rows_ref[n : n + 1, :] = jnp.full((1, LANES), value, f32)


def ready_kernel(
    count,
    width,
    own_far_ref,
    own_near_ref,
    near_ref,
    far_ref,
    order_ref,
    cells_ref,
    column_ref,
):
    even = lax.axis_index(PLACE) % 2 == 0

    def fill(*refs):
        for t in range(count):
            rows = [load_row(ref, count, width, t, r) for ref in refs for r in range(width)]
            for r, row in enumerate(rows):
                cells_ref[t, r] = row
            if t == 0:
                for r in range(len(rows) - 2 * (width - 1)):
                    column_ref[r] = rows[r + width - 1]

    @pl.when(even)
    def _():
        fill(far_ref, own_far_ref, own_near_ref, near_ref)

    @pl.when(jnp.logical_not(even))
    def _():
        fill(near_ref, own_near_ref, own_far_ref, far_ref)


def scalar_rows(count, heats):
    rows = count * (count + 2 + heats) + 2 * heats
    return -(-rows // SUB) * SUB


class Scalars:
    def __init__(self, ref, count, heats):
        self.ref, self.count, self.heats = ref, count, heats

    def row(self, n):
        return jnp.broadcast_to(self.ref[n : n + 1, :], (SUB, LANES))

    def kinetics(self, i, j):
        return self.row(i * self.count + j)

    def photolysis(self, i):
        return self.row(self.count * self.count + i)

    def weight(self, k, i):
        return self.row(self.count * (self.count + 1 + k) + i)

    def mixed_yield(self, i):
        return self.row(self.count * (self.count + 1 + self.heats) + i)

    def heat_yield(self, k):
        return self.row(self.count * (self.count + 2 + self.heats) + k)

    def heat_mixed_yield(self, k):
        return self.row(self.count * (self.count + 2 + self.heats) + self.heats + k)

    def quad(self, size):
        first = scalar_rows(self.count, self.heats)
        return self.ref[first : first + size, :][:, :1]


def cut(value):
    return [value[:, j : j + LANES] for j in range(0, value.shape[1], LANES)]


def combine(factors, values):
    total = [factors[0] * tile for tile in values[0]]
    for factor, value in zip(factors[1:], values[1:]):
        total = [old + factor * tile for old, tile in zip(total, value)]
    return total


def stencil(coeffs, r, centre, north, south):
    return (
        coeffs[0, r] * centre
        + coeffs[1, r] * shift(centre, True)
        + coeffs[2, r] * shift(centre, False)
        + coeffs[3, r] * north
        + coeffs[4, r] * south
    )


def substeps_kernel(
    heats,
    rows_ref,
    received_ref,
    cells_ref,
    table_ref,
    turn_ref,
    coeffs_ref,
    base_ref,
    lead_ref,
    second_lead_ref,
    heat_ref,
    warm_ref,
    middle,
):
    count, depth, _, span = cells_ref.shape
    rows = lead_ref.shape[0]
    band = rows - 2
    margin = (SUB - band) // 2
    halo = (depth - band) // 2
    waves = table_ref.shape[0] // 8
    fields = 4
    place = lax.axis_index(PLACE)
    places = lax.axis_size(PLACE)
    scalars = Scalars(rows_ref, count, heats)

    lane = lax.broadcasted_iota(jnp.int32, (SUB, 8 * waves), 1)
    real = (lane // waves) % 2 == 0
    turn_cos, turn_sin = turn_ref[0], turn_ref[1]
    scale = 1.0 / math.sqrt(waves)
    turn_a = jnp.where(real, turn_cos, turn_sin) * scale
    turn_b = jnp.where(real, -turn_sin, turn_cos) * scale
    turned = jnp.concatenate([received_ref[...]] * 8, axis=0).T
    wanted = [(f, r) for f in range(fields - 1) for r in range(-1, band + 1)]
    wanted += [(fields - 1, r) for r in range(band)]
    left = []
    for f, r in wanted:
        at = f * SUB + margin + r
        re = turned[at : at + 1]
        im = turned[fields * SUB + at : fields * SUB + at + 1]
        left.append(re * turn_a + im * turn_b)
    left = jnp.concatenate(left, axis=0)
    high, low = split_bf16(left)
    whole_lane = lax.broadcasted_iota(jnp.int32, left.shape, 1)
    left = jnp.where(whole_lane < 4 * waves, high.astype(f32), low).astype(bf16)
    grid = jnp.dot(left, table_ref[...], preferred_element_type=f32)

    for r in range(rows):
        across = grid[r * SUB : (r + 1) * SUB]
        along = grid[(rows + r) * SUB : (rows + r + 1) * SUB]
        warmth = grid[(2 * rows + r) * SUB : (2 * rows + r + 1) * SUB]
        courant_x = 0.45 * jnp.tanh(across)
        courant_y = 0.45 * jnp.tanh(along)
        own = 1.0 - jnp.abs(courant_x) - jnp.abs(courant_y)
        if r == 0 or r == rows - 1:
            inside = (place > 0) if r == 0 else (place < places - 1)
            courant_x = jnp.where(inside, courant_x, 0.0)
            courant_y = jnp.where(inside, courant_y, 0.0)
            own = jnp.where(inside, own, 0.0)
        coeffs_ref[0, r] = own
        coeffs_ref[1, r] = jnp.maximum(courant_x, 0.0)
        coeffs_ref[2, r] = -jnp.minimum(courant_x, 0.0)
        coeffs_ref[3, r] = jnp.maximum(courant_y, 0.0)
        coeffs_ref[4, r] = -jnp.minimum(courant_y, 0.0)
        coeffs_ref[5, r] = 0.2 * jnp.exp(0.3 * warmth)
    first = 3 * rows * SUB
    for r in range(band):
        warm_ref[r] = 1.0 + 0.5 * jnp.tanh(grid[first + r * SUB : first + (r + 1) * SUB])

    for r in range(rows):
        at = r + halo - 1
        moved = [
            stencil(coeffs_ref, r, cells_ref[t, at], cells_ref[t, at - 1], cells_ref[t, at + 1])
            for t in range(count)
        ]
        lead_ref[r] = moved[0]
        moved = [cut(value) for value in moved]
        rate = cut(coeffs_ref[5, r])
        for i in range(count):
            mixed = combine([scalars.kinetics(i, j) for j in range(count)], moved)
            out = [a + b * c for a, b, c in zip(moved[i], rate, mixed)]
            middle[i, r] = jnp.concatenate(out, axis=1)

    for r in range(band):
        moved = [
            stencil(coeffs_ref, r + 1, middle[t, r + 1], middle[t, r], middle[t, r + 2])
            for t in range(count)
        ]
        second_lead_ref[r] = moved[0]
        moved = [cut(value) for value in moved]
        rate = cut(coeffs_ref[5, r + 1])
        outs = []
        for i in range(count):
            mixed = combine([scalars.kinetics(i, j) for j in range(count)], moved)
            outs.append([a + b * c for a, b, c in zip(moved[i], rate, mixed)])
            base_ref[i, r] = jnp.concatenate(outs[i], axis=1)
        for k in range(heats):
            total = combine([scalars.weight(k, i) for i in range(count)], outs)
            heat_ref[k, r] = jnp.concatenate(total, axis=1)


def analysis_kernel(
    levels,
    count,
    rows_ref,
    above_ref,
    turned_ref,
    turn_ref,
    coeffs_ref,
    lead_ref,
    second_lead_ref,
    heat_ref,
    warm_ref,
    u_ref,
    v_ref,
    sent_ref,
):
    rows, _, span = lead_ref.shape
    band = rows - 2
    heats = heat_ref.shape[0]
    waves = turned_ref.shape[1] // 8
    lons = span * SUB
    scalars = Scalars(rows_ref, count, heats)
    turn_cos, turn_sin = turn_ref[0], turn_ref[1]
    covered = lax.axis_index("lev") > 0
    photo, source = [], []
    for r in range(rows):
        overhead = jnp.where(covered, above_ref[r], 0.0)
        photo.append(0.2 * jnp.exp(overhead * (-2.0 / levels)))
        source.append(photo[r] * lead_ref[r])

    heated = [[None] * band for _ in range(heats)]
    for r in range(band):
        moved = cut(stencil(coeffs_ref, r + 1, source[r + 1], source[r], source[r + 2]))
        rate, light = cut(coeffs_ref[5, r + 1]), cut(photo[r + 1])
        own = scalars.photolysis(0)
        v = [a * b for a, b in zip(rate, moved)]
        lead = cut(second_lead_ref[r])
        u = [m + p * (a + own * m) for m, p, a in zip(moved, light, lead)]
        u_ref[r] = jnp.concatenate(u, axis=1)
        v_ref[r] = jnp.concatenate(v, axis=1)
        for k in range(heats):
            by_u, by_v = scalars.heat_yield(k), scalars.heat_mixed_yield(k)
            parts = cut(heat_ref[k, r])
            parts = [a + by_u * b + by_v * c for a, b, c in zip(parts, u, v)]
            heated[k][r] = jnp.concatenate(parts, axis=1) * warm_ref[r]

    heat = jnp.concatenate([row for group in heated for row in group], axis=0)
    high, low = split_bf16(heat)
    by_high = jnp.dot(high, turned_ref[...], preferred_element_type=f32)
    by_low = jnp.dot(low.astype(bf16), turned_ref[...], preferred_element_type=f32)
    wide = 8 * waves
    total = by_high + pltpu.roll(by_high, wide - 2 * waves, 1) + by_low
    sums_a, sums_b = [], []
    for n in range(heats * band):
        part = total[n * SUB : (n + 1) * SUB]
        sums_a.append(jnp.sum(part * turn_cos, axis=0, keepdims=True))
        sums_b.append(jnp.sum(part * turn_sin, axis=0, keepdims=True))
    pad = -len(sums_a) % SUB
    sums_a += [jnp.zeros_like(sums_a[0])] * pad
    sums_b += [jnp.zeros_like(sums_b[0])] * pad
    sums_a = jnp.concatenate(sums_a, axis=0)
    sums_b = jnp.concatenate(sums_b, axis=0)
    other = pltpu.roll(sums_b, wide - waves, 1)
    re = sums_a + other
    im = pltpu.roll(sums_a, wide - waves, 1) - sums_b
    size = re.shape[0]
    quad = scalars.quad(size)
    both = jnp.concatenate([re, im], axis=0) * (1.0 / math.sqrt(lons))
    both = both * jnp.concatenate([quad, quad], axis=0)
    filler = jnp.zeros((LANES - 2 * size, wide), f32)
    sent_ref[...] = jnp.concatenate([both, filler], axis=0).T[:waves]


def last_kernel(
    band,
    heats,
    received_ref,
    legendre_ref,
    rows_ref,
    base_ref,
    u_ref,
    v_ref,
    spectra_hbm,
    flat_hbm,
    spread,
    spectra_ref,
    flat_ref,
    sems,
):
    places = received_ref.shape[0]
    count = base_ref.shape[0]
    received = received_ref[...]
    for r in range(band):
        spread[pl.ds(r, places, stride=band), :] = pltpu.roll(received, (LANES - r) % LANES, 1)
    size = -(-heats * band // SUB) * SUB
    weighted = spread[...].T[: 2 * size].astype(bf16)
    out = jnp.dot(weighted, legendre_ref[...], preferred_element_type=f32)
    for p in range(2):
        for k in range(heats):
            at = p * size + k * band
            spectra_ref[p, k, 0] = out[at : at + 1]
    copies = [pltpu.make_async_copy(spectra_ref, spectra_hbm, sems.at[count])]
    copies[0].start()
    scalars = Scalars(rows_ref, count, heats)
    each = flat_hbm.shape[0] // count
    for t in range(count):
        by_u, by_v = scalars.photolysis(t), scalars.mixed_yield(t)
        for r in range(band):
            parts = zip(cut(base_ref[t, r]), cut(u_ref[r]), cut(v_ref[r]))
            store_row(flat_ref, count, band, t, r, [a + by_u * b + by_v * c for a, b, c in parts])
        mine = pl.ds(t * each, each)
        copies.append(pltpu.make_async_copy(flat_ref.at[mine], flat_hbm.at[mine], sems.at[t]))
        copies[-1].start()
    for copy in copies:
        copy.wait()


def body(spectra, legendre, wavenumbers, quad_weights, tracers, kinetics, photolysis, heat_weights):
    places = lax.axis_size(PLACE)
    levels = lax.axis_size("lev")
    count, _, band, lons = tracers.shape
    waves = wavenumbers.shape[0]
    heats = heat_weights.shape[0]
    lats, degrees = legendre.shape[2], legendre.shape[1]
    width = band // 2
    span = lons // SUB
    flat_rows = count * band * lons // LANES
    VM, SM = pltpu.VMEM, pltpu.SMEM
    legendre_t = legendre[0].T
    shape = jax.ShapeDtypeStruct

    near_pairs = [(i, i ^ 1) for i in range(places)]
    far_pairs = [(i, ((i + 1) ^ 1) - 1) for i in range(1, places - 1)]

    half = shape((count * lons // LANES, band // 2, LANES), f32)
    own_near, own_far, waves_in, spectra_in, legendre_in = call(
        edges_kernel,
        [
            half,
            half,
            shape((1, waves), jnp.int32),
            shape((*spectra.shape[:2], degrees), bf16),
            shape((lats, degrees), bf16),
        ],
        [pltpu.HBM] * 4,
        [pltpu.SemaphoreType.DMA((5,))],
    )(
        *(
            pltpu.with_memory_space_constraint(x, pltpu.HBM)
            for x in (
                wavenumbers.reshape(1, waves),
                spectra[:, :, 0, 0],
                legendre_t,
                halves(tracers[:, 0]),
            )
        )
    )
    own_far, own_near = own_far.reshape(-1, LANES), own_near.reshape(-1, LANES)
    near = lax.ppermute(own_near, PLACE, near_pairs)
    far = lax.ppermute(own_far, PLACE, far_pairs)
    sent, masked = call(
        functools.partial(fourier_kernel, band),
        [shape((places, LANES), f32), shape((lats, degrees), bf16)],
        [VM] * 3,
        [pltpu.VMEM((lats + 2 * SUB, LANES), f32)],
        flops=1000000,
    )(waves_in, spectra_in, legendre_in)
    received = lax.all_to_all(sent, PLACE, 0, 0, tiled=True)

    constants = scalar_rows(count, heats)
    table, turned, turn, scalars = call(
        table_kernel,
        [
            shape((8 * waves, span), bf16),
            shape((span, 8 * waves), bf16),
            shape((2, SUB, 8 * waves), f32),
            shape((constants + 2 * SUB, LANES), f32),
        ],
        [SM] * 5 + [pl.ANY],
        flops=20000000000,
    )(wavenumbers, kinetics, photolysis, heat_weights, quad_weights, sent)

    cells, column = call(
        functools.partial(ready_kernel, count, width),
        [
            shape((count, band + 2 * width, SUB, span), f32),
            shape((band + 2, SUB, span), f32),
        ],
        [VM] * 4 + [pl.ANY],
    )(own_far, own_near, near, far, sent)
    above = lax.ppermute(column, "lev", [(i, (i + 1) % levels) for i in range(levels)])
    if levels > 2:
        above = jnp.where(lax.axis_index("lev") > 0, above, 0.0)
    reach = 1
    while reach < levels - 1:
        above = above + lax.ppermute(
            above, "lev", [(i, i + reach) for i in range(levels - reach)]
        )
        reach *= 2

    inner, outer = (band, SUB, span), (band + 2, SUB, span)
    coeffs, base, lead, second_lead, heat, warm = call(
        functools.partial(substeps_kernel, heats),
        [
            shape((6, *outer), f32),
            shape((count, *inner), f32),
            shape(outer, f32),
            shape(inner, f32),
            shape((heats, *inner), f32),
            shape(inner, f32),
        ],
        [VM] * 5,
        [pltpu.VMEM((count, *outer), f32)],
    )(scalars, received, cells, table, turn)
    u, v, heat_sent = call(
        functools.partial(analysis_kernel, levels, count),
        [shape(inner, f32), shape(inner, f32), shape((waves, LANES), f32)],
        [VM] * 9,
    )(scalars, above, turned, turn, coeffs, lead, second_lead, heat, warm)
    heat_received = lax.all_to_all(heat_sent, PLACE, 0, 0, tiled=True)
    heating_spectra, flat_out = call(
        functools.partial(last_kernel, band, heats),
        [shape((2, heats, 1, 1, degrees), f32), shape((flat_rows, LANES), f32)],
        [VM] * 6,
        [
            pltpu.VMEM((lats, LANES), f32),
            pltpu.VMEM((2, heats, 1, 1, degrees), f32),
            pltpu.VMEM((flat_rows, LANES), f32),
            pltpu.SemaphoreType.DMA((count + 1,)),
        ],
        out_space=pltpu.HBM,
    )(heat_received, masked, scalars, base, u, v)
    return (unfold(flat_out, count, band)[:, None], heating_spectra)


def solution(mesh):
    return jax.shard_map(
        body,
        mesh=mesh,
        in_specs=(
            P(None, None, "lev", ("wave", "grp"), None),
            P(("wave", "grp"), None, None),
            P(),
            P(),
            P(None, "lev", ("wave", "grp"), None),
            P(),
            P(),
            P(),
        ),
        out_specs=(
            P(None, "lev", ("wave", "grp"), None),
            P(None, None, "lev", ("wave", "grp"), None),
        ),
        check_vma=False,
    )
```
